128 devices in a mesh: seq: 8 (over z, core), ch: 16 (over y, x).
Axes of the slice: x: 4, y: 4, z: 4, core: 2. Of those that a mesh axis runs over, the one named last changes fastest.
Arguments:
- tokens: bfloat16 [2, 1024, 2048], P(None, 'seq'), may hold values from -6 to 6
- cotangent: bfloat16 [2, 1024, 2048], P(None, 'seq'), may hold values from -6 to 6
- short_lengths: int32 [8], replicated, may hold values from 1 to 898, 1024 in all
- long_lengths: int32 [3], replicated, may hold values from 1 to 898, 1024 in all
- gain_one: float32 [2048], replicated, may hold values from 0.25 to 1.75
- gain_two: float32 [2048], replicated, may hold values from 0.25 to 1.75
- w_y: bfloat16 [2048, 2736], P(None, 'ch'), may hold values from -0.125 to 0.125
- w_x: bfloat16 [2048, 2736], P(None, 'ch'), may hold values from -0.125 to 0.125
- conv_w: float32 [4, 2736], P(None, 'ch'), may hold values from -3 to 3
- conv_b: float32 [2736], P('ch'), may hold values from -0.5 to 0.5
- gate_a: bfloat16 [16, 171, 171], P('ch'), may hold values from -0.4375 to 0.4375
- gate_x: bfloat16 [16, 171, 171], P('ch'), may hold values from -0.4375 to 0.4375
- bias_a: float32 [2736], P('ch'), may hold values from -1 to 1
- bias_x: float32 [2736], P('ch'), may hold values from -1 to 1
- lam: float32 [2736], P('ch'), may hold values from 4 to 12
- w_out: bfloat16 [2736, 2048], P('ch'), may hold values from -0.3125 to 0.3125
- w_one: bfloat16 [2048, 6144], P(None, 'ch'), may hold values from -0.125 to 0.125
- w_two: bfloat16 [2048, 6144], P(None, 'ch'), may hold values from -0.125 to 0.125
- w_three: bfloat16 [6144, 2048], P('ch'), may hold values from -0.15625 to 0.15625
Outputs:
- layer_out: bfloat16 [2, 1024, 2048], P(None, 'seq')
- d_tokens: float32 [2, 1024, 2048], P(None, 'seq')
- g_gain_one: float32 [2048], P('ch')
- g_gain_two: float32 [2048], P('ch')
- g_w_y: float32 [2048, 2736], P(None, 'ch')
- g_w_x: float32 [2048, 2736], P(None, 'ch')
- g_conv_w: float32 [4, 2736], P(None, 'ch')
- g_conv_b: float32 [2736], P('ch')
- g_gate_a: float32 [16, 171, 171], P('ch')
- g_gate_x: float32 [16, 171, 171], P('ch')
- g_bias_a: float32 [2736], P('ch')
- g_bias_x: float32 [2736], P('ch')
- g_lam: float32 [2736], P('ch')
- g_w_out: float32 [2736, 2048], P('ch')
- g_w_one: float32 [2048, 6144], P(None, 'ch')
- g_w_two: float32 [2048, 6144], P(None, 'ch')
- g_w_three: float32 [6144, 2048], P('ch')
The draws below stay inside these ranges and needn't reach their ends.
Inputs may be any that keep to these rules, and one draw needn't show every extreme that they name: `short_lengths`: each row's document lengths sum to 1024 and the longest has exactly 898 positions. `long_lengths`: each row's document lengths sum to 1024 and the longest has exactly 898 positions.
All inputs are finite; a program needn't handle non-finite values.
Results may differ from the reference program's by a relative error of at most 0.023.
Values may be sent and summed in bfloat16 or wider, within the bound.
No kernel may reach another device: no remote copies, remote signals or barrier semaphores. Data moves between devices by JAX's collectives and lax.ppermute only.
A program may use at most 128 MiB of HBM per device.

```python
import math
from functools import partial
import jax
import jax.numpy as jnp
import numpy as np
from jax import lax

D = 2048
RNN = 2736
FF = 6144
CONV = 4
BLOCKS = 16
BW = 171
GROUPS = 2
SHORT_DOCS = 8
LONG_DOCS = 3
TOKENS_ROW = 1024
SPAN = 898


def draw_lam(key, part):
    key = jax.random.fold_in(key, 11)
    lower_end = 0.5 / TOKENS_ROW
    upper_end = 0.012
    spread = jax.random.uniform(key, (RNN,), jnp.float32)
    decay_rate = jnp.exp(jnp.log(lower_end) + spread * (jnp.log(upper_end) - jnp.log(lower_end)))
    return -jnp.log(jnp.expm1(decay_rate))


def shard_levels(stream_key, extent, shards, low, top_value):
    loudness = 1.0
    for dim, shards_of in shards:
        steps = jax.random.uniform(jax.random.fold_in(jax.random.fold_in(stream_key, 6), dim), (shards_of,), jnp.float32, low / len(shards), top_value / len(shards))
        loudness = loudness * jnp.repeat(jnp.exp(steps), extent[dim] // shards_of).reshape((-1,) + (1,) * (len(extent) - 1 - dim))
    return loudness


def length_profile(count, total, limit, lean):
    loads = [(1 << 20) // math.isqrt(grade ** lean) + 1 for grade in range(2, count + 1)]
    rest, counts = total - limit - (count - 1), [1] * (count - 1)
    while rest > 0:
        movable = [i for i in range(count - 1) if counts[i] < limit]
        whole, remaining = sum([loads[i] for i in movable]), rest
        for i in movable:
            more = min(limit - counts[i], max(1, remaining * loads[i] // whole), rest)
            counts[i] = counts[i] + more
            rest = rest - more
    return np.array([limit] + counts)


def uneven(stream_key, count, total, most, skew):
    if count == 2:
        one = jax.random.randint(stream_key, (), max(1, total - most), min(most, total - 1) + 1)
        return jnp.stack([one, total - one])
    tallies = jnp.asarray(length_profile(count, total, most, skew), jnp.int32)
    couples = (count - 1) // 2
    giver, taker = tallies[1:1 + 2 * couples:2], tallies[2:2 + 2 * couples:2]
    room = jnp.minimum(giver - 1, most - taker)
    shifted = jax.random.randint(jax.random.fold_in(stream_key, 1), (couples,), 0, 1 << 20) % (room + 1)
    tallies = tallies.at[1:1 + 2 * couples:2].set(giver - shifted).at[2:2 + 2 * couples:2].set(taker + shifted)
    return tallies[jax.random.permutation(jax.random.fold_in(stream_key, 2), count)]


def normal_values(stream_key, extent, scale, limit, shards=(), held_as=jnp.bfloat16):
    gain = shard_levels(stream_key, extent, shards, -0.22, 0.18) if shards else 1.0
    drawn = jax.random.normal(stream_key, extent, jnp.float32) * scale * gain
    return jnp.minimum(jnp.maximum(drawn, -limit), limit).astype(held_as)


def setup_inputs(seed: int = 0) -> dict:
    splits = jax.random.split(jax.random.key(seed), 20)
    tokens = normal_values(splits[0], (GROUPS, TOKENS_ROW, D), 1.0, 6.0, ((1, 8),))
    cotangent = normal_values(splits[1], (GROUPS, TOKENS_ROW, D), 1.0, 6.0, ((1, 8),))
    short_lengths = uneven(splits[2], SHORT_DOCS, TOKENS_ROW, SPAN, 0).astype(jnp.int32)
    long_lengths = uneven(splits[3], LONG_DOCS, TOKENS_ROW, SPAN, 0).astype(jnp.int32)
    gain_one = jnp.clip(1.0 + 0.15 * jax.random.normal(splits[4], (D,), jnp.float32), 0.25, 1.75)
    gain_two = jnp.clip(1.0 + 0.15 * jax.random.normal(splits[5], (D,), jnp.float32), 0.25, 1.75)
    w_y = normal_values(splits[6], (D, RNN), D ** -0.5, 0.125, ((1, 16),))
    w_x = normal_values(splits[7], (D, RNN), D ** -0.5, 0.125, ((1, 16),))
    conv_w = normal_values(splits[8], (CONV, RNN), 0.5, 3.0, ((1, 16),), jnp.float32)
    conv_b = jnp.clip(jax.random.uniform(splits[9], (RNN,), jnp.float32, -0.5, 0.5) * shard_levels(splits[9], (RNN,), ((0, 16),), -0.4, 0.0), -0.5, 0.5)
    gate_a = normal_values(splits[10], (BLOCKS, BW, BW), BW ** -0.5, 0.4375, ((0, 16),))
    gate_x = normal_values(splits[11], (BLOCKS, BW, BW), BW ** -0.5, 0.4375, ((0, 16),))
    bias_a = jnp.clip(jax.random.uniform(splits[12], (RNN,), jnp.float32, -1.0, 1.0) * shard_levels(splits[12], (RNN,), ((0, 16),), -0.4, 0.0), -1.0, 1.0)
    bias_x = jnp.clip(jax.random.uniform(splits[13], (RNN,), jnp.float32, -1.0, 1.0) * shard_levels(splits[13], (RNN,), ((0, 16),), -0.4, 0.0), -1.0, 1.0)
    lam = draw_lam(jax.random.fold_in(splits[19], 71), 0)
    w_out = normal_values(splits[15], (RNN, D), (RNN // 8) ** -0.5, 0.3125, ((0, 16),))
    w_one = normal_values(splits[16], (D, FF), D ** -0.5, 0.125, ((1, 16),))
    w_two = normal_values(splits[17], (D, FF), D ** -0.5, 0.125, ((1, 16),))
    w_three = normal_values(splits[18], (FF, D), (FF // 4) ** -0.5, 0.15625, ((0, 16),))
    return dict(tokens=tokens, cotangent=cotangent, short_lengths=short_lengths, long_lengths=long_lengths, gain_one=gain_one, gain_two=gain_two, w_y=w_y, w_x=w_x, conv_w=conv_w, conv_b=conv_b, gate_a=gate_a, gate_x=gate_x, bias_a=bias_a, bias_x=bias_x, lam=lam, w_out=w_out, w_one=w_one, w_two=w_two, w_three=w_three)


@jax.custom_vjp
def low(v):
    return lax.optimization_barrier(v.astype(jnp.bfloat16)).astype(jnp.float32)

@jax.custom_vjp
def low_back(v):
    return v

def low_keep(v):
    return (low(v), None)

def low_pass(kept, grad):
    return (grad,)

def back_keep(v):
    return (v, None)

def back_low(kept, grad):
    return (low(grad),)
low.defvjp(low_keep, low_pass)
low_back.defvjp(back_keep, back_low)
EPS_NORM = 1e-06

def matmul(left, right, form):
    return jnp.einsum(form, left, right, precision=lax.Precision.HIGHEST)

def doc_index(lengths, positions):
    doc_ends = jnp.cumsum(lengths)
    return lax.optimization_barrier(jnp.sum((positions[:, None] >= doc_ends[None, :]).astype(jnp.int32), axis=1))

def doc_masks(lengths, positions, width):
    doc_ids = doc_index(lengths, positions)
    result = [jnp.ones(positions.shape, jnp.float32)]
    for offset in range(1, width):
        before = doc_index(lengths, positions - offset)
        result.append(((positions - offset >= 0) & (doc_ids == before)).astype(jnp.float32))
    return jnp.stack(result)

def rms_scale(features, gain_vec):
    inverse = lax.rsqrt(lax.optimization_barrier(jnp.mean(features * features, axis=-1, keepdims=True)) + EPS_NORM)
    return features * inverse * gain_vec

def recurrence_inputs(raw_a, raw_x, conv_out, lam, bias_a, bias_x, reset):
    rate_gate = jax.nn.sigmoid(raw_a + bias_a)
    inlet_gate = jax.nn.sigmoid(raw_x + bias_x)
    log_decay = -8.0 * jax.nn.softplus(-lam) * rate_gate
    keep_gate = jnp.exp(log_decay) * reset
    drive_term = jnp.sqrt(-jnp.expm1(2.0 * log_decay)) * inlet_gate * conv_out
    return (keep_gate, drive_term)

def forward(tokens_f, gain_one, gain_two, w_y, w_x, conv_w, conv_b, gate_a, gate_x, bias_a, bias_x, lam, w_out, w_one, w_two, w_three, same_masks):
    group_count, row_total, _ = tokens_f.shape
    normed_one = low(rms_scale(tokens_f, gain_one))
    gate_pre = low_back(matmul(normed_one, w_y, 'gtd,dc->gtc'))
    gate_branch = jax.nn.gelu(gate_pre, approximate=True)
    conv_input = low(low_back(matmul(normed_one, w_x, 'gtd,dc->gtc')))
    padded = jnp.pad(conv_input, ((0, 0), (CONV - 1, 0), (0, 0)))
    conv_out = conv_b + jnp.zeros_like(conv_input)
    for offset in range(CONV):
        conv_out = conv_out + conv_w[offset] * padded[:, CONV - 1 - offset:CONV - 1 - offset + row_total] * same_masks[offset][..., None]
    conv_low = low(conv_out).reshape(group_count, row_total, BLOCKS, BW)
    raw_a = low_back(matmul(conv_low, gate_a, 'gtbi,bij->gtbj')).reshape(group_count, row_total, RNN)
    raw_x = low_back(matmul(conv_low, gate_x, 'gtbi,bij->gtbj')).reshape(group_count, row_total, RNN)
    keep_gate, drive_term = recurrence_inputs(raw_a, raw_x, conv_out, lam, bias_a, bias_x, same_masks[1][..., None])

    def advance(carried, step_pair):
        carried = step_pair[0] * carried + step_pair[1]
        return (carried, carried)
    _, states = lax.scan(advance, jnp.zeros((group_count, RNN), jnp.float32), (jnp.swapaxes(keep_gate, 0, 1), jnp.swapaxes(drive_term, 0, 1)))
    state_seq = jnp.swapaxes(states, 0, 1)
    mixed_in = low(state_seq * gate_branch)
    resid_mid = tokens_f + low_back(matmul(mixed_in, w_out, 'gtc,cd->gtd'))
    normed_two = low(rms_scale(resid_mid, gain_two))
    mlp_gate = low_back(matmul(normed_two, w_one, 'gtd,df->gtf'))
    mlp_up = low_back(matmul(normed_two, w_two, 'gtd,df->gtf'))
    mlp_hidden = low(jax.nn.gelu(mlp_gate, approximate=True) * mlp_up)
    return low(resid_mid + matmul(mlp_hidden, w_three, 'gtf,fd->gtd'))

def reference(tokens, cotangent, short_lengths, long_lengths, gain_one, gain_two, w_y, w_x, conv_w, conv_b, gate_a, gate_x, bias_a, bias_x, lam, w_out, w_one, w_two, w_three):
    positions = jnp.arange(TOKENS_ROW, dtype=jnp.int32)
    same_masks = jnp.stack([doc_masks(short_lengths, positions, CONV), doc_masks(long_lengths, positions, CONV)], axis=1)
    f32 = jnp.float32
    layer_out, pull = jax.vjp(partial(forward, same_masks=same_masks), tokens.astype(f32), gain_one, gain_two, w_y.astype(f32), w_x.astype(f32), conv_w, conv_b, gate_a.astype(f32), gate_x.astype(f32), bias_a, bias_x, lam, w_out.astype(f32), w_one.astype(f32), w_two.astype(f32), w_three.astype(f32))
    grads = pull(cotangent.astype(f32))
    return (layer_out.astype(jnp.bfloat16), grads[0], grads[1], grads[2], grads[3], grads[4], grads[5], grads[6], grads[7], grads[8], grads[9], grads[10], grads[11], grads[12], grads[13], grads[14], grads[15])
```

```python
from functools import partial

import jax
import jax.numpy as jnp
from jax import lax
from jax.experimental import pallas as pl
from jax.experimental.pallas import tpu as pltpu
from jax.sharding import PartitionSpec as P

EPS_NORM = 1e-06
F32 = jnp.float32
BF16 = jnp.bfloat16
TAPS = 4
HALO = 8


def dot(left, right, contract):
    return lax.dot_general(left, right, (contract, ((), ())), preferred_element_type=F32)


def expm1_neg(x):
    series = x * (
        1.0
        + x * (1 / 2)
        * (1.0 + x * (1 / 3) * (1.0 + x * (1 / 4) * (1.0 + x * (1 / 5) * (1.0 + x * (1 / 6) * (1.0 + x * (1 / 7))))))
    )
    return jnp.where(x > -0.35, series, jnp.exp(x) - 1.0)


def doc_masks(ends, count, start, rows):
    positions = start + lax.broadcasted_iota(jnp.int32, (rows, 1), 0)

    def doc(at):
        total = jnp.zeros((rows, 1), jnp.int32)
        for j in range(count):
            total = total + (at >= ends[j]).astype(jnp.int32)
        return total

    here = doc(positions)
    masks = [jnp.ones((rows, 1), F32)]
    for k in range(1, TAPS):
        same = (here == doc(positions - k)) & (positions >= k)
        masks.append(same.astype(F32))
    return masks


def row_ends(length_ref, count):
    ends, total = [], 0
    for j in range(count):
        total = total + length_ref[j]
        ends.append(total)
    return ends


def forward_kernel(
    start_ref,
    short_ref,
    long_ref,
    conv_in_ref,
    edge_ref,
    conv_w_ref,
    conv_b_ref,
    gate_a_ref,
    gate_x_ref,
    bias_a_ref,
    bias_x_ref,
    decay_ref,
    conv_out_ref,
    rate_ref,
    inlet_ref,
    keep_ref,
    run_ref,
    state_ref,
    carry_ref,
    ext,
):
    groups, rows, chans = conv_in_ref.shape
    for g in range(groups):
        length_ref = (short_ref, long_ref)[g]
        count = length_ref.shape[0]
        masks = doc_masks(row_ends(length_ref, count), count, start_ref[0], rows)
        ext[g, HALO - TAPS + 1 : HALO, :] = edge_ref[g].astype(F32)
        ext[g, HALO:, :] = conv_in_ref[g].astype(F32)
        conv_out = jnp.broadcast_to(conv_b_ref[...], (rows, chans))
        for k in range(TAPS):
            conv_out = (
                conv_out + conv_w_ref[k : k + 1, :] * ext[g, HALO - k : HALO - k + rows, :] * masks[k]
            )
        conv_out_ref[g] = conv_out
        low = conv_out.astype(BF16)
        rate = jax.nn.sigmoid(dot(low, gate_a_ref[0], ((1,), (0,))) + bias_a_ref[...])
        inlet = jax.nn.sigmoid(dot(low, gate_x_ref[0], ((1,), (0,))) + bias_x_ref[...])
        rate_ref[g] = rate
        inlet_ref[g] = inlet
        log_decay = decay_ref[...] * rate
        keep_ref[g] = jnp.exp(log_decay) * masks[1]
        state_ref[g] = jnp.sqrt(-expm1_neg(2.0 * log_decay)) * inlet * conv_out

    def step(t, carried):
        out = []
        for g in range(groups):
            run, state = carried[g]
            keep = keep_ref[g, pl.ds(t, 1), :]
            run = run * keep
            state = state * keep + state_ref[g, pl.ds(t, 1), :]
            run_ref[g, pl.ds(t, 1), :] = run
            state_ref[g, pl.ds(t, 1), :] = state
            out.append((run, state))
        return tuple(out)

    first = tuple((jnp.ones((1, chans), F32), jnp.zeros((1, chans), F32)) for _ in range(groups))
    last = lax.fori_loop(0, rows, step, first, unroll=8)
    for g in range(groups):
        carry_ref[0, g : g + 1, :] = last[g][0]
        carry_ref[1, g : g + 1, :] = last[g][1]


def gelu_parts(x):
    root = 0.7978845608028654
    cubic = 0.044715
    inner = root * (x + cubic * x * x * x)
    th = jnp.tanh(inner)
    half = 0.5 * (1.0 + th)
    slope = half + 0.5 * x * (1.0 - th * th) * root * (1.0 + 3.0 * cubic * x * x)
    return x * half, slope


def adjoint_kernel(
    d_mixed_ref,
    gate_pre_ref,
    hidden_ref,
    keep_ref,
    d_gate_pre_ref,
    reach_ref,
    adj_ref,
    carry_ref,
):
    groups, rows, chans = d_mixed_ref.shape
    for g in range(groups):
        branch, slope = gelu_parts(gate_pre_ref[g])
        d_mixed = d_mixed_ref[g]
        d_gate_pre_ref[g] = (d_mixed * hidden_ref[g] * slope).astype(BF16)
        adj_ref[g] = d_mixed * branch

    def step(i, carried):
        t = rows - 1 - i
        out = []
        for g in range(groups):
            reach, passed = carried[g]
            adj = adj_ref[g, pl.ds(t, 1), :] + passed
            adj_ref[g, pl.ds(t, 1), :] = adj
            reach_ref[g, pl.ds(t, 1), :] = reach
            keep = keep_ref[g, pl.ds(t, 1), :]
            out.append((reach * keep, adj * keep))
        return tuple(out)

    first = tuple((jnp.ones((1, chans), F32), jnp.zeros((1, chans), F32)) for _ in range(groups))
    last = lax.fori_loop(0, rows, step, first, unroll=8)
    for g in range(groups):
        carry_ref[0, g : g + 1, :] = last[g][0]
        carry_ref[1, g : g + 1, :] = last[g][1]


def gates_back_kernel(
    start_ref,
    short_ref,
    long_ref,
    adj_ref,
    reach_ref,
    beyond_ref,
    state_in_ref,
    hidden_ref,
    keep_ref,
    rate_ref,
    inlet_ref,
    conv_out_ref,
    conv_in_ref,
    edge_ref,
    conv_w_ref,
    gate_a_ref,
    gate_x_ref,
    decay_ref,
    lam_slope_ref,
    d_conv_head_ref,
    d_input_ref,
    g_gate_a_ref,
    g_gate_x_ref,
    g_rows_ref,
    ext,
    prior,
    d_ext,
):
    groups, rows, chans = adj_ref.shape
    sums = [jnp.zeros((1, chans), F32) for _ in range(8)]
    for g in range(groups):
        length_ref = (short_ref, long_ref)[g]
        count = length_ref.shape[0]
        ends = row_ends(length_ref, count)
        masks = doc_masks(ends, count, start_ref[0], rows)
        adjoint = adj_ref[g] + reach_ref[g] * beyond_ref[g : g + 1, :]
        prior[HALO - 1 : HALO, :] = state_in_ref[g : g + 1, :]
        prior[HALO:, :] = hidden_ref[g]
        d_keep = adjoint * prior[HALO - 1 : HALO - 1 + rows, :]
        rate = rate_ref[g]
        inlet = inlet_ref[g]
        conv_out = conv_out_ref[g]
        decay = decay_ref[...]
        log_decay = decay * rate
        square = -expm1_neg(2.0 * log_decay)
        root = jnp.sqrt(square)
        driven = adjoint * conv_out
        d_log = d_keep * keep_ref[g] - driven * inlet * (1.0 - square) / root
        d_rate_pre = d_log * decay * rate * (1.0 - rate)
        d_inlet_pre = driven * root * inlet * (1.0 - inlet)
        sums[0] = sums[0] + jnp.sum(d_rate_pre, axis=0, keepdims=True)
        sums[1] = sums[1] + jnp.sum(d_inlet_pre, axis=0, keepdims=True)
        sums[2] = sums[2] + jnp.sum(d_log * rate, axis=0, keepdims=True)
        low = conv_out.astype(BF16)
        low_a = d_rate_pre.astype(BF16)
        low_x = d_inlet_pre.astype(BF16)
        grad_a = dot(low, low_a, ((0,), (0,)))
        grad_x = dot(low, low_x, ((0,), (0,)))
        if g == 0:
            g_gate_a_ref[...] = grad_a
            g_gate_x_ref[...] = grad_x
        else:
            g_gate_a_ref[...] += grad_a
            g_gate_x_ref[...] += grad_x
        d_conv = (
            adjoint * root * inlet
            + dot(low_a, gate_a_ref[0], ((1,), (1,)))
            + dot(low_x, gate_x_ref[0], ((1,), (1,)))
        )
        sums[3] = sums[3] + jnp.sum(d_conv, axis=0, keepdims=True)
        ext[HALO - TAPS + 1 : HALO, :] = edge_ref[g].astype(F32)
        ext[HALO:, :] = conv_in_ref[g].astype(F32)
        d_input = conv_w_ref[0:1, :] * d_conv
        sums[4] = sums[4] + jnp.sum(d_conv * ext[HALO:, :], axis=0, keepdims=True)
        d_ext[rows:, :] = jnp.zeros((HALO, chans), F32)
        for k in range(1, TAPS):
            masked = d_conv * masks[k]
            sums[4 + k] = sums[4 + k] + jnp.sum(
                masked * ext[HALO - k : HALO - k + rows, :], axis=0, keepdims=True
            )
            d_ext[:rows, :] = masked
            d_input = d_input + conv_w_ref[k : k + 1, :] * d_ext[k : k + rows, :]
        d_input_ref[g] = d_input
        d_conv_head_ref[g] = d_conv[: TAPS - 1, :]
    sums[2] = sums[2] * lam_slope_ref[...]
    for i, total in enumerate(sums):
        g_rows_ref[i : i + 1, :] = total


def sds(shape, dtype=F32):
    return jax.ShapeDtypeStruct(shape, dtype)


def run_kernel(kernel, name, outs, ins, scratch=(), flops=0, smem=0):
    vmem = pl.BlockSpec(memory_space=pltpu.VMEM)
    scalar = pl.BlockSpec(memory_space=pltpu.SMEM)
    moved = sum(a.size * a.dtype.itemsize for a in list(ins) + list(outs))
    return pl.pallas_call(
        kernel,
        name=name,
        out_shape=outs,
        in_specs=[scalar] * smem + [vmem] * (len(ins) - smem),
        out_specs=[vmem] * len(outs),
        scratch_shapes=list(scratch),
        cost_estimate=pl.CostEstimate(flops=flops, bytes_accessed=moved, transcendentals=0),
        compiler_params=pltpu.CompilerParams(vmem_limit_bytes=32 * 1024 * 1024),
    )(*ins)


def shifted(block, axis, distance):
    count = lax.axis_size(axis)
    route = [(i - distance, i) for i in range(count) if 0 <= i - distance < count]
    return lax.ppermute(block, axis, route)


def gather_small(value, axis):
    count = lax.axis_size(axis)
    return lax.all_to_all(jnp.broadcast_to(value[None], (count,) + value.shape), axis, 0, 0)


def carried_in(value, axis, backward):
    count, mine = lax.axis_size(axis), lax.axis_index(axis)
    pieces = gather_small(value, axis)
    total = jnp.zeros(value.shape[1:], F32)
    order = range(count - 1, 0, -1) if backward else range(count - 1)
    for j in order:
        longer = pieces[j, 1] + pieces[j, 0] * total
        total = jnp.where((j > mine) if backward else (j < mine), longer, total)
    return total


def scatter_rows(partial_sum, extra=None):
    count = lax.axis_size("ch")
    rows, width = partial_sum.shape
    pieces = partial_sum.astype(BF16).reshape(count, rows // count, width)
    if extra is not None:
        extra = jnp.pad(extra.astype(BF16).reshape(count, 1, -1), ((0, 0), (0, rows // count - 1), (0, 0)))
        pieces = jnp.concatenate([pieces, extra], axis=-1)
    got = lax.all_to_all(pieces, "ch", 0, 0)
    total = jnp.sum(got.astype(F32), axis=0)
    if extra is not None:
        return total[:, :width], total[0, width:]
    return total


def gather_rows(share):
    count = lax.axis_size("ch")
    got = lax.all_to_all(jnp.broadcast_to(share[None], (count,) + share.shape), "ch", 0, 0)
    return got.reshape(count * share.shape[0], share.shape[1])


def seq_scatter(bundle):
    return lax.psum_scatter(bundle.astype(BF16), "seq", scatter_dimension=0, tiled=True)


def seq_gather(share):
    return lax.all_gather(share, "seq", axis=0, tiled=True)


def rms(features):
    return lax.rsqrt(jnp.mean(features * features, axis=-1, keepdims=True) + EPS_NORM)


def norm_back(features, scale, gain, grad):
    gained = gain * grad
    mean = jnp.mean(gained * features, axis=-1, keepdims=True)
    return scale * gained - features * (scale * scale * scale) * mean


def body(
    tokens,
    cotangent,
    short_lengths,
    long_lengths,
    gain_one,
    gain_two,
    w_y,
    w_x,
    conv_w,
    conv_b,
    gate_a,
    gate_x,
    bias_a,
    bias_x,
    lam,
    w_out,
    w_one,
    w_two,
    w_three,
):
    groups, rows, width = tokens.shape
    chans = w_x.shape[1]
    hidden_units = w_one.shape[1]
    total_rows = groups * rows
    ch_count, ch_index = lax.axis_size("ch"), lax.axis_index("ch")
    seq_count, seq_index = lax.axis_size("seq"), lax.axis_index("seq")
    share_rows = total_rows // ch_count
    share_width = width // ch_count
    start = (seq_index * rows).astype(jnp.int32)[None]
    grouped = lambda a: a.reshape(groups, rows, a.shape[-1])
    mine = lambda a: lax.dynamic_slice_in_dim(a, ch_index * share_rows, share_rows, 0)

    tokens = tokens.reshape(total_rows, width)
    cotangent = cotangent.reshape(total_rows, width)
    tokens_f = tokens.astype(F32)
    scale_one = rms(tokens_f)
    normed_one = (tokens_f * scale_one * gain_one).astype(BF16)
    conv_input = grouped(dot(normed_one, w_x, ((1,), (0,))).astype(BF16))
    edge = shifted(conv_input[:, rows - TAPS + 1 :], "seq", 1)
    gate_pre = grouped(dot(normed_one, w_y, ((1,), (0,))))

    decay = (-8.0 * jax.nn.softplus(-lam))[None]
    lam_slope = (8.0 * jax.nn.sigmoid(-lam))[None]
    big = sds((groups, rows, chans))
    flops = 2 * total_rows * chans * chans
    conv_out, rate, inlet, keep, decay_run, local_state, carry = run_kernel(
        forward_kernel,
        "conv_gates_scan",
        [big] * 6 + [sds((2, groups, chans))],
        [
            start,
            short_lengths,
            long_lengths,
            conv_input,
            edge,
            conv_w,
            conv_b[None],
            gate_a,
            gate_x,
            bias_a[None],
            bias_x[None],
            decay,
        ],
        [pltpu.VMEM((groups, HALO + rows, chans), F32)],
        flops=2 * flops,
        smem=3,
    )
    state_in = carried_in(carry, "seq", False)
    hidden = local_state + decay_run * state_in[:, None]
    mixed_in = (hidden * jax.nn.gelu(gate_pre, approximate=True)).astype(BF16)
    mixed_in = mixed_in.reshape(total_rows, chans)
    mix_share = scatter_rows(dot(mixed_in, w_out, ((1,), (0,))))
    resid_share = mine(tokens_f) + mix_share
    scale_two = rms(resid_share)
    normed_two = gather_rows((resid_share * scale_two * gain_two).astype(BF16))

    mlp_gate = dot(normed_two, w_one, ((1,), (0,)))
    mlp_up = dot(normed_two, w_two, ((1,), (0,)))
    gate_value, gate_slope = gelu_parts(mlp_gate)
    mlp_hidden = (gate_value * mlp_up).astype(BF16)
    d_hidden = dot(cotangent, w_three, ((1,), (1,)))
    d_gate = (d_hidden * mlp_up * gate_slope).astype(BF16)
    d_up = (d_hidden * gate_value).astype(BF16)
    partial_two = dot(d_gate, w_one, ((1,), (1,))) + dot(d_up, w_two, ((1,), (1,)))
    gain_two_share = resid_share * scale_two
    sum_two = scatter_rows(partial_two)
    gain_two_part = jnp.sum(sum_two * gain_two_share, axis=0)
    d_mid = mine(cotangent.astype(F32)) + norm_back(resid_share, scale_two, gain_two, sum_two)
    d_mix = gather_rows(d_mid.astype(BF16))

    g_mlp = jnp.concatenate(
        [
            dot(normed_two, d_gate, ((0,), (0,))).astype(BF16),
            dot(normed_two, d_up, ((0,), (0,))).astype(BF16),
            dot(cotangent, mlp_hidden, ((0,), (0,))).astype(BF16),
        ],
        axis=1,
    )
    g_mlp = seq_gather(seq_scatter(g_mlp))

    d_mixed = grouped(dot(d_mix, w_out, ((1,), (1,))))
    d_gate_pre, reach, local_adjoint, carry_back = run_kernel(
        adjoint_kernel,
        "adjoint_scan",
        [sds((groups, rows, chans), BF16), big, big, sds((2, groups, chans))],
        [d_mixed, gate_pre, hidden, keep],
    )
    beyond = carried_in(carry_back, "seq", True)
    d_conv_head, d_input, g_gate_a, g_gate_x, g_rows = run_kernel(
        gates_back_kernel,
        "gates_back",
        [
            sds((groups, TAPS - 1, chans)),
            big,
            sds((chans, chans)),
            sds((chans, chans)),
            sds((8, chans)),
        ],
        [
            start,
            short_lengths,
            long_lengths,
            local_adjoint,
            reach,
            beyond,
            state_in,
            hidden,
            keep,
            rate,
            inlet,
            conv_out,
            conv_input,
            edge,
            conv_w,
            gate_a,
            gate_x,
            decay,
            lam_slope,
        ],
        [
            pltpu.VMEM((HALO + rows, chans), F32),
            pltpu.VMEM((HALO + rows, chans), F32),
            pltpu.VMEM((rows + HALO, chans), F32),
        ],
        flops=4 * flops,
        smem=3,
    )
    lead = shifted(d_conv_head, "seq", -1)
    ahead = start[0] + rows + jnp.arange(TAPS - 1, dtype=jnp.int32)
    lead_masks = []
    for lengths in (short_lengths, long_lengths):
        ends = jnp.cumsum(lengths)
        doc = lambda at: jnp.sum((at[:, None] >= ends[None, :]).astype(jnp.int32), axis=1)
        lead_masks.append(jnp.stack([(doc(ahead) == doc(ahead - k)).astype(F32) for k in range(TAPS)]))
    lead_masks = jnp.stack(lead_masks)
    late = []
    for i in range(TAPS - 1):
        total = jnp.zeros((groups, chans), F32)
        for k in range(TAPS):
            j = i + k - (TAPS - 1)
            if j >= 0:
                total = total + conv_w[k] * lead_masks[:, k, j, None] * lead[:, j]
        late.append(total)
    late = jnp.pad(jnp.stack(late, axis=1), ((0, 0), (rows - TAPS + 1, 0), (0, 0)))
    d_input = (d_input + late).astype(BF16).reshape(total_rows, chans)
    d_gate_pre = d_gate_pre.reshape(total_rows, chans)

    partial_one = dot(d_input, w_x, ((1,), (1,))) + dot(d_gate_pre, w_y, ((1,), (1,)))
    gain_one_part = jnp.sum(partial_one * (tokens_f * scale_one), axis=0)
    sum_one, g_gain_one = scatter_rows(partial_one, gain_one_part)
    tokens_share = mine(tokens_f)
    d_tokens = d_mid + norm_back(tokens_share, mine(scale_one), gain_one, sum_one)
    d_tokens = grouped(gather_rows(d_tokens.astype(BF16)).astype(F32))

    gain_two_got = lax.all_to_all(gain_two_part.reshape(ch_count, share_width), "ch", 0, 0)
    g_gain_two = jnp.sum(gain_two_got, axis=0)

    partial_out = dot(mlp_hidden, w_three, ((1,), (0,)))
    out_share = resid_share + scatter_rows(partial_out)
    layer_out = grouped(gather_rows(out_share.astype(BF16)))

    g_mid = jnp.concatenate(
        [
            dot(normed_one, d_gate_pre, ((0,), (0,))).astype(BF16),
            dot(d_mix, mixed_in, ((0,), (0,))).astype(BF16),
        ],
        axis=1,
    )
    g_mid = seq_gather(seq_scatter(g_mid))

    g_w_x = dot(normed_one, d_input, ((0,), (0,)))
    gains = jnp.pad(jnp.stack([g_gain_one, g_gain_two]), ((0, 0), (0, chans - share_width)))
    tail = jnp.concatenate([g_w_x, g_gate_a, g_gate_x, g_rows, gains], axis=0).astype(BF16)
    tail_rows = tail.shape[0]
    tail = jnp.pad(tail, ((0, -tail_rows % (16 * seq_count)), (0, 0)))
    tail = seq_gather(seq_scatter(tail)).astype(F32)
    at = width
    g_gate_a = tail[at : at + chans][None]
    g_gate_x = tail[at + chans : at + 2 * chans][None]
    at = at + 2 * chans
    return (
        layer_out,
        d_tokens,
        tail[at + 8, :share_width],
        tail[at + 9, :share_width],
        g_mid[:, :chans].astype(F32),
        tail[:width],
        tail[at + 4 : at + 8],
        tail[at + 3],
        g_gate_a,
        g_gate_x,
        tail[at],
        tail[at + 1],
        tail[at + 2],
        g_mid[:, chans:].astype(F32).T,
        g_mlp[:, :hidden_units].astype(F32),
        g_mlp[:, hidden_units : 2 * hidden_units].astype(F32),
        g_mlp[:, 2 * hidden_units :].astype(F32).T,
    )


def solution(mesh):
    tokens_spec = P(None, "seq", None)
    column = P(None, "ch")
    block = P("ch", None, None)
    row = P("ch", None)
    vector = P("ch")
    return jax.shard_map(
        body,
        mesh=mesh,
        in_specs=(
            tokens_spec,
            tokens_spec,
            P(),
            P(),
            P(),
            P(),
            column,
            column,
            column,
            vector,
            block,
            block,
            vector,
            vector,
            vector,
            row,
            column,
            column,
            row,
        ),
        out_specs=(
            tokens_spec,
            tokens_spec,
            vector,
            vector,
            column,
            column,
            column,
            vector,
            block,
            block,
            vector,
            vector,
            vector,
            row,
            column,
            column,
            row,
        ),
        check_vma=False,
    )
```

```python
import math

import jax
import jax.numpy as jnp
from jax import lax
from jax.experimental import pallas as pl
from jax.experimental.pallas import tpu as pltpu
from jax.sharding import PartitionSpec as P

EPS_NORM = 1e-06
F32 = jnp.float32
BF16 = jnp.bfloat16
TAPS = 4
VMEM_LIMIT = 16 * 1024 * 1024
LANES = 256
GATE_ROWS = 24
SMALL_ROWS = 64
WIDE = 512
GAIN_ROWS = 16
HBM_PER_US = 3_600_000
HALO = 8


def dot(left, right, contract):
    return lax.dot_general(left, right, (contract, ((), ())), preferred_element_type=F32)


def expm1_neg(x):
    series = x * (
        1.0
        + x * (1 / 2)
        * (1.0 + x * (1 / 3) * (1.0 + x * (1 / 4) * (1.0 + x * (1 / 5) * (1.0 + x * (1 / 6) * (1.0 + x * (1 / 7))))))
    )
    return jnp.where(x > -0.35, series, jnp.exp(x) - 1.0)


def doc_masks(ends, count, start, rows):
    positions = start + lax.broadcasted_iota(jnp.int32, (rows, 1), 0)

    def doc(at):
        total = jnp.zeros((rows, 1), jnp.int32)
        for j in range(count):
            total = total + (at >= ends[j]).astype(jnp.int32)
        return total

    here = doc(positions)
    masks = [jnp.ones((rows, 1), F32)]
    for k in range(1, TAPS):
        same = (here == doc(positions - k)) & (positions >= k)
        masks.append(same.astype(F32))
    return masks


def row_ends(length_ref, count):
    ends, total = [], 0
    for j in range(count):
        total = total + length_ref[j]
        ends.append(total)
    return ends


def forward_kernel(
    start_ref,
    short_ref,
    long_ref,
    conv_in_ref,
    edge_ref,
    conv_w_ref,
    conv_b_ref,
    gate_a_ref,
    gate_x_ref,
    bias_a_ref,
    bias_x_ref,
    decay_ref,
    conv_out_ref,
    rate_ref,
    inlet_ref,
    keep_ref,
    run_ref,
    state_ref,
    carry_ref,
    ext,
):
    groups, rows, chans = conv_in_ref.shape
    for g in range(groups):
        length_ref = (short_ref, long_ref)[g]
        count = length_ref.shape[0]
        masks = doc_masks(row_ends(length_ref, count), count, start_ref[0], rows)
        ext[g, HALO - TAPS + 1 : HALO, :] = edge_ref[g].astype(F32)
        ext[g, HALO:, :] = conv_in_ref[g].astype(F32)
        conv_out = jnp.broadcast_to(conv_b_ref[...], (rows, chans))
        for k in range(TAPS):
            conv_out = (
                conv_out + conv_w_ref[k : k + 1, :] * ext[g, HALO - k : HALO - k + rows, :] * masks[k]
            )
        conv_out_ref[g] = conv_out
        low = conv_out.astype(BF16)
        rate = jax.nn.sigmoid(dot(low, gate_a_ref[0], ((1,), (0,))) + bias_a_ref[...])
        inlet = jax.nn.sigmoid(dot(low, gate_x_ref[0], ((1,), (0,))) + bias_x_ref[...])
        rate_ref[g] = rate
        inlet_ref[g] = inlet
        log_decay = decay_ref[...] * rate
        keep_ref[g] = jnp.exp(log_decay) * masks[1]
        state_ref[g] = jnp.sqrt(-expm1_neg(2.0 * log_decay)) * inlet * conv_out

    def step(t, carried):
        out = []
        for g in range(groups):
            run, state = carried[g]
            keep = keep_ref[g, pl.ds(t, 1), :]
            run = run * keep
            state = state * keep + state_ref[g, pl.ds(t, 1), :]
            run_ref[g, pl.ds(t, 1), :] = run
            state_ref[g, pl.ds(t, 1), :] = state
            out.append((run, state))
        return tuple(out)

    first = tuple((jnp.ones((1, chans), F32), jnp.zeros((1, chans), F32)) for _ in range(groups))
    last = lax.fori_loop(0, rows, step, first, unroll=8)
    for g in range(groups):
        carry_ref[0, g : g + 1, :] = last[g][0]
        carry_ref[1, g : g + 1, :] = last[g][1]


def gelu_parts(x):
    root = 0.7978845608028654
    cubic = 0.044715
    inner = root * (x + cubic * x * x * x)
    th = jnp.tanh(inner)
    half = 0.5 * (1.0 + th)
    slope = half + 0.5 * x * (1.0 - th * th) * root * (1.0 + 3.0 * cubic * x * x)
    return x * half, slope


def adjoint_kernel(
    d_mixed_ref,
    gate_pre_ref,
    hidden_ref,
    keep_ref,
    d_gate_pre_ref,
    reach_ref,
    adj_ref,
    carry_ref,
):
    groups, rows, chans = d_mixed_ref.shape
    for g in range(groups):
        branch, slope = gelu_parts(gate_pre_ref[g])
        d_mixed = d_mixed_ref[g]
        d_gate_pre_ref[g] = (d_mixed * hidden_ref[g] * slope).astype(BF16)
        adj_ref[g] = d_mixed * branch

    def step(i, carried):
        t = rows - 1 - i
        out = []
        for g in range(groups):
            reach, passed = carried[g]
            adj = adj_ref[g, pl.ds(t, 1), :] + passed
            adj_ref[g, pl.ds(t, 1), :] = adj
            reach_ref[g, pl.ds(t, 1), :] = reach
            keep = keep_ref[g, pl.ds(t, 1), :]
            out.append((reach * keep, adj * keep))
        return tuple(out)

    first = tuple((jnp.ones((1, chans), F32), jnp.zeros((1, chans), F32)) for _ in range(groups))
    last = lax.fori_loop(0, rows, step, first, unroll=8)
    for g in range(groups):
        carry_ref[0, g : g + 1, :] = last[g][0]
        carry_ref[1, g : g + 1, :] = last[g][1]


def gates_back_kernel(
    midway,
    start_ref,
    short_ref,
    long_ref,
    adj_ref,
    reach_ref,
    beyond_ref,
    state_in_ref,
    hidden_ref,
    keep_ref,
    rate_ref,
    inlet_ref,
    conv_out_ref,
    conv_in_ref,
    edge_ref,
    conv_w_ref,
    gate_a_ref,
    gate_x_ref,
    decay_ref,
    lam_slope_ref,
    d_conv_head_ref,
    d_input_ref,
    small_ref,
    ext,
    prior,
    d_ext,
):
    groups, rows, chans = adj_ref.shape
    sums = [jnp.zeros((1, chans), F32) for _ in range(8)]
    grad_a = grad_x = jnp.zeros((chans, chans), F32)
    for g in range(groups):
        length_ref = (short_ref, long_ref)[g]
        count = length_ref.shape[0]
        ends = row_ends(length_ref, count)
        masks = doc_masks(ends, count, start_ref[0], rows)
        adjoint = adj_ref[g] + reach_ref[g] * beyond_ref[g : g + 1, :]
        prior[HALO - 1 : HALO, :] = state_in_ref[g : g + 1, :]
        prior[HALO:, :] = hidden_ref[g]
        d_keep = adjoint * prior[HALO - 1 : HALO - 1 + rows, :]
        rate = rate_ref[g]
        inlet = inlet_ref[g]
        conv_out = conv_out_ref[g]
        decay = decay_ref[...]
        log_decay = decay * rate
        square = -expm1_neg(2.0 * log_decay)
        root = jnp.sqrt(square)
        driven = adjoint * conv_out
        d_log = d_keep * keep_ref[g] - driven * inlet * (1.0 - square) / root
        d_rate_pre = d_log * decay * rate * (1.0 - rate)
        d_inlet_pre = driven * root * inlet * (1.0 - inlet)
        sums[0] = sums[0] + jnp.sum(d_rate_pre, axis=0, keepdims=True)
        sums[1] = sums[1] + jnp.sum(d_inlet_pre, axis=0, keepdims=True)
        sums[2] = sums[2] + jnp.sum(d_log * rate, axis=0, keepdims=True)
        low = conv_out.astype(BF16)
        low_a = d_rate_pre.astype(BF16)
        low_x = d_inlet_pre.astype(BF16)
        grad_a = grad_a + dot(low, low_a, ((0,), (0,)))
        grad_x = grad_x + dot(low, low_x, ((0,), (0,)))
        d_conv = (
            adjoint * root * inlet
            + dot(low_a, gate_a_ref[0], ((1,), (1,)))
            + dot(low_x, gate_x_ref[0], ((1,), (1,)))
        )
        sums[3] = sums[3] + jnp.sum(d_conv, axis=0, keepdims=True)
        ext[HALO - TAPS + 1 : HALO, :] = edge_ref[g].astype(F32)
        ext[HALO:, :] = conv_in_ref[g].astype(F32)
        d_input = conv_w_ref[0:1, :] * d_conv
        sums[4] = sums[4] + jnp.sum(d_conv * ext[HALO:, :], axis=0, keepdims=True)
        d_ext[rows:, :] = jnp.zeros((HALO, chans), F32)
        for k in range(1, TAPS):
            masked = d_conv * masks[k]
            sums[4 + k] = sums[4 + k] + jnp.sum(
                masked * ext[HALO - k : HALO - k + rows, :], axis=0, keepdims=True
            )
            d_ext[:rows, :] = masked
            d_input = d_input + conv_w_ref[k : k + 1, :] * d_ext[k : k + rows, :]
        d_input_ref[g] = d_input
        d_conv_head_ref[g] = d_conv[: TAPS - 1, :]
        if g == 0:
            midway()
    sums[2] = sums[2] * lam_slope_ref[...]
    small_ref[...] = jnp.zeros(small_ref.shape, F32)
    for i, total in enumerate(sums):
        lanes = slice(LANES * i, LANES * i + chans)
        first, last = GATE_ROWS * i, min(GATE_ROWS * (i + 1), chans)
        small_ref[: last - first, lanes] = grad_a[first:last]
        small_ref[GATE_ROWS : GATE_ROWS + last - first, lanes] = grad_x[first:last]
        small_ref[2 * GATE_ROWS : 2 * GATE_ROWS + 1, lanes] = total


def sds(shape, dtype=F32):
    return jax.ShapeDtypeStruct(shape, dtype)


def in_hbm(array):
    return pltpu.with_memory_space_constraint(array, pltpu.HBM)


def run_kernel(kernel, name, outs, ins, scratch=(), flops=0, smem=0, after=(), passed=None, waits=0):
    vmem = pl.BlockSpec(memory_space=pltpu.VMEM)
    scalar = pl.BlockSpec(memory_space=pltpu.SMEM)
    anywhere = pl.BlockSpec(memory_space=pl.ANY)
    moved = sum(a.size * a.dtype.itemsize for a in list(ins) + list(outs))
    count, skip = len(ins), len(after)
    ins = [*ins, *[in_hbm(a) for a in after]]
    in_specs = [scalar] * smem + [vmem] * (count - smem) + [anywhere] * skip
    out_specs = [vmem] * len(outs)
    outs, scratch = list(outs), list(scratch)
    if passed is not None:
        ins.append(in_hbm(passed))
        in_specs.append(anywhere)
        outs.append(pltpu.HBM(passed.shape, passed.dtype))
        out_specs.append(anywhere)
        scratch += [pltpu.VMEM(passed.shape, passed.dtype), pltpu.SemaphoreType.DMA((2,))]

    def run(*refs):
        if passed is None:
            kernel(*refs[:count], *refs[count + skip :])
            return
        in_ref, out_ref = refs[count + skip], refs[count + skip + len(outs)]
        held, sems = refs[-2:]
        fetch = pltpu.make_async_copy(in_ref, held, sems.at[0])
        store = pltpu.make_async_copy(held, out_ref, sems.at[1])
        fetch.start()

        def midway():
            fetch.wait()
            store.start()

        kept = refs[count + skip + 1 : count + skip + len(outs)]
        kernel(midway, *refs[:count], *kept, *refs[count + skip + len(outs) + 1 : -2])
        store.wait()

    return pl.pallas_call(
        run,
        name=name,
        out_shape=outs,
        in_specs=in_specs,
        out_specs=out_specs,
        scratch_shapes=scratch,
        cost_estimate=pl.CostEstimate(flops=flops, bytes_accessed=moved + waits * HBM_PER_US, transcendentals=0),
        compiler_params=pltpu.CompilerParams(vmem_limit_bytes=VMEM_LIMIT),
    )(*ins)


def shifted(block, axis, distance):
    count = lax.axis_size(axis)
    route = [(i - distance, i) for i in range(count) if 0 <= i - distance < count]
    return lax.ppermute(block, axis, route)


def carried_in(value, backward):
    count, mine = lax.axis_size("seq"), lax.axis_index("seq")
    pieces = lax.all_to_all(jnp.broadcast_to(value[None], (count,) + value.shape), "seq", 0, 0)
    total = jnp.zeros(value.shape[1:], F32)
    for j in range(count - 1, 0, -1) if backward else range(count - 1):
        longer = pieces[j, 1] + pieces[j, 0] * total
        total = jnp.where((j > mine) if backward else (j < mine), longer, total)
    return total


def sum_parts(got_ref):
    total = got_ref[0].astype(F32)
    for j in range(1, got_ref.shape[0]):
        total = total + got_ref[j].astype(F32)
    return total


def send_to_all(out_ref, share):
    share = share.astype(BF16)
    for j in range(out_ref.shape[0]):
        out_ref[j] = share


def norm_back(features, gain, grad):
    scale = rms(features)
    gained = gain * grad
    mean = jnp.mean(gained * features, axis=-1, keepdims=True)
    back = scale * gained - features * (scale * scale * scale) * mean
    return back, jnp.sum(grad * (features * scale), axis=0, keepdims=True)


def mid_kernel(got_ref, tokens_ref, gain_ref, resid_ref, normed_ref):
    resid = tokens_ref[...].astype(F32) + sum_parts(got_ref)
    resid_ref[...] = resid
    send_to_all(normed_ref, resid * rms(resid) * gain_ref[...])


def mid_back_kernel(got_ref, resid_ref, cotangent_ref, gain_ref, d_mid_ref, g_gain_ref, d_mix_ref):
    back, g_gain = norm_back(resid_ref[...], gain_ref[...], sum_parts(got_ref))
    d_mid = cotangent_ref[...].astype(F32) + back
    d_mid_ref[...] = d_mid
    g_gain_ref[...] = g_gain
    send_to_all(d_mix_ref, d_mid)


def tokens_back_kernel(got_ref, tokens_ref, resid_ref, d_mid_ref, gain_ref, *refs):
    *chunk_refs, both_ref, sent_ref = refs
    width = tokens_ref.shape[1]
    total = sum_parts(got_ref)
    rows, lanes = chunk_refs[0].shape
    chunk = chunk_refs[0][...].astype(F32)
    for chunk_ref in chunk_refs[1:]:
        chunk = chunk + chunk_ref[...].astype(F32)
    gains = total[:GAIN_ROWS, 2 * width :]
    sent_ref[:rows, :] = chunk.astype(BF16)
    sent_ref[rows:, : gains.shape[1]] = gains.astype(BF16)
    sent_ref[rows:, gains.shape[1] :] = jnp.zeros((GAIN_ROWS, lanes - gains.shape[1]), BF16)
    back, _ = norm_back(tokens_ref[...].astype(F32), gain_ref[...], total[:, :width])
    d_tokens = (d_mid_ref[...] + back).astype(BF16)
    layer_out = (resid_ref[...] + total[:, width : 2 * width]).astype(BF16)
    for j in range(both_ref.shape[0]):
        both_ref[j, 0] = d_tokens
        both_ref[j, 1] = layer_out


def split_both(both, after):
    owners, _, share, width = both.shape

    def run(both_ref, after_ref, d_tokens_ref, layer_ref):
        d_tokens_ref[...] = both_ref[:, 0].astype(F32)
        layer_ref[...] = both_ref[:, 1]

    part = pl.BlockSpec((owners, share, WIDE), lambda i: (0, 0, i))
    return pl.pallas_call(
        run,
        name="split_both",
        grid=(width // WIDE,),
        in_specs=[
            pl.BlockSpec((owners, 2, share, WIDE), lambda i: (0, 0, 0, i)),
            pl.BlockSpec(memory_space=pl.ANY),
        ],
        out_specs=[part, part],
        out_shape=[pltpu.HBM((owners, share, width), F32), pltpu.HBM((owners, share, width), BF16)],
        cost_estimate=pl.CostEstimate(flops=0, bytes_accessed=5 * both.size, transcendentals=0),
        compiler_params=pltpu.CompilerParams(vmem_limit_bytes=VMEM_LIMIT),
    )(both, in_hbm(after))


def exchange(pieces):
    return lax.all_to_all(pieces, "ch", 0, 0)


def by_owner(partial_sum):
    count = lax.axis_size("ch")
    rows, width = partial_sum.shape
    return partial_sum.astype(BF16).reshape(count, rows // count, width)


def with_gains(pieces, gains):
    count, share, width = pieces[0].shape
    more = gains.astype(BF16).reshape(-1, count, width // count).swapaxes(0, 1)
    more = jnp.pad(more, ((0, 0), (0, share - gains.shape[0]), (0, 0)))
    return jnp.concatenate([*pieces, more], axis=-1)


def seq_route(fn):
    count = lax.axis_size("seq")
    return [(i, fn(i) % count) for i in range(count)]


def swap_core(value):
    return lax.ppermute(value, "seq", seq_route(lambda i: i ^ 1))


def shift_z(value, hops):
    return lax.ppermute(value, "seq", seq_route(lambda i: i + 2 * hops))


def half_of(array, axis, other):
    core = lax.axis_index("seq") % 2
    size = array.shape[axis] // 2
    return lax.dynamic_slice_in_dim(array, ((1 - core) if other else core) * size, size, axis)


def reduce_chunk(kept, sent, axis):
    z = lax.axis_index("seq") // 2
    got = swap_core(sent.astype(BF16))
    size = kept.shape[axis] // 4

    def piece(hops):
        at = ((z + hops) % 4) * size
        cut = lambda a: lax.dynamic_slice_in_dim(a, at, size, axis).astype(F32)
        return (cut(kept) + cut(got)).astype(BF16)

    return [piece(0)] + [shift_z(piece(hops), hops) for hops in (1, 3, 2)]


def assemble(kernel, name, chunks, outs, specs, after):
    def out_spec(block, dim):
        return pl.BlockSpec(
            block, lambda i: tuple(i % 2 * 4 + i // 2 if d == dim else 0 for d in range(len(block)))
        )

    def run(chunks_ref, *refs):
        kernel(chunks_ref[0], *refs[len(after) :])

    return pl.pallas_call(
        run,
        name=name,
        grid=(chunks.shape[0],),
        in_specs=[pl.BlockSpec((1,) + chunks.shape[1:], lambda i: (i, 0, 0))]
        + [pl.BlockSpec(memory_space=pl.ANY)] * len(after),
        out_specs=[out_spec(*spec) for spec in specs],
        out_shape=outs,
        cost_estimate=pl.CostEstimate(
            flops=0, bytes_accessed=2 * chunks.size + sum(4 * math.prod(o.shape) for o in outs), transcendentals=0
        ),
        compiler_params=pltpu.CompilerParams(vmem_limit_bytes=VMEM_LIMIT),
    )(chunks, *[in_hbm(a) for a in after])


def place_chunk(piece, y_ref, out_ref, x_ref, gate_a_ref, gate_x_ref, rows_ref, gains_ref):
    chans = x_ref.shape[0]
    piece = piece.astype(F32)
    size = (piece.shape[0] - SMALL_ROWS - GAIN_ROWS) // 3
    y_ref[...] = piece[:chans]
    out_ref[...] = piece[size : size + chans]
    x_ref[...] = piece[2 * size : 2 * size + chans]
    at = 3 * size
    gate_a_ref[0] = piece[at : at + GATE_ROWS, :chans]
    gate_x_ref[0] = piece[at + GATE_ROWS : at + 2 * GATE_ROWS, :chans]
    rows_ref[0] = piece[at + 2 * GATE_ROWS : at + 2 * GATE_ROWS + 8]
    gains = piece[at + SMALL_ROWS : at + SMALL_ROWS + 8]

    @pl.when(pl.program_id(0) == 0)
    def _():
        gains_ref[...] = gains

    @pl.when(pl.program_id(0) > 0)
    def _():
        gains_ref[...] += gains


def mlp_kernel(normed_ref, d_hidden_ref, one_hbm, two_hbm, cot_hbm, parts_ref, hidden_ref, grads_hbm, one, two, cot, grads, sems):
    owners, share, width = parts_ref.shape
    units = one.shape[1]
    fetches = [
        pltpu.make_async_copy(source, held, sems.at[n])
        for n, (source, held) in enumerate(((one_hbm, one), (two_hbm, two), (cot_hbm, cot)))
    ]
    for fetch in fetches:
        fetch.start()
    normed = normed_ref[...]
    fetches[0].wait()
    value, slope = gelu_parts(dot(normed, one[...], ((1,), (0,))))
    fetches[1].wait()
    up = dot(normed, two[...], ((1,), (0,)))
    d_hidden = d_hidden_ref[...]
    hidden = (value * up).astype(BF16)
    d_gate = (d_hidden * up * slope).astype(BF16)
    d_up = (d_hidden * value).astype(BF16)
    hidden_ref[...] = hidden
    for at in range(0, width, WIDE):
        cols = slice(at, at + WIDE)
        back = dot(d_gate, one[cols, :], ((1,), (1,))) + dot(d_up, two[cols, :], ((1,), (1,)))
        parts_ref[:, :, cols] = back.astype(BF16).reshape(owners, share, WIDE)
    fetches[2].wait()
    stores = []
    for n, at in enumerate(range(0, width, WIDE)):
        cols = slice(at, at + WIDE)
        part = normed_ref[:, cols]
        grads[cols, :units] = dot(part, d_gate, ((0,), (0,))).astype(BF16)
        grads[cols, units : 2 * units] = dot(part, d_up, ((0,), (0,))).astype(BF16)
        grads[cols, 2 * units :] = dot(cot[:, cols], hidden, ((0,), (0,))).astype(BF16)
        stores.append(pltpu.make_async_copy(grads.at[cols], grads_hbm.at[cols], sems.at[3 + n]))
        stores[-1].start()
    for store in stores:
        store.wait()


def mlp_back(normed, d_hidden, w_one, w_two, cotangent, owners):
    rows, width = normed.shape
    units = w_one.shape[1]
    vmem = pl.BlockSpec(memory_space=pltpu.VMEM)
    anywhere = pl.BlockSpec(memory_space=pl.ANY)
    return pl.pallas_call(
        mlp_kernel,
        name="mlp",
        in_specs=[vmem, vmem, anywhere, anywhere, anywhere],
        out_specs=[vmem, vmem, anywhere],
        out_shape=[
            sds((owners, rows // owners, width), BF16),
            sds((rows, units), BF16),
            pltpu.HBM((width, 3 * units), BF16),
        ],
        scratch_shapes=[
            pltpu.VMEM((width, units), BF16),
            pltpu.VMEM((width, units), BF16),
            pltpu.VMEM((rows, width), BF16),
            pltpu.VMEM((width, 3 * units), BF16),
            pltpu.SemaphoreType.DMA((3 + width // WIDE,)),
        ],
        cost_estimate=pl.CostEstimate(
            flops=14 * rows * width * units, bytes_accessed=14 * width * units, transcendentals=0
        ),
        compiler_params=pltpu.CompilerParams(vmem_limit_bytes=2 * VMEM_LIMIT),
    )(normed, d_hidden, in_hbm(w_one), in_hbm(w_two), in_hbm(cotangent))


def place_mlp(bundle, units):
    width = bundle.shape[0]

    def run(piece_ref, one_ref, two_ref, three_ref):
        one_ref[...] = piece_ref[:, :units].astype(F32)
        two_ref[...] = piece_ref[:, units : 2 * units].astype(F32)
        three_ref[...] = piece_ref[:, 2 * units :].astype(F32).T

    block = pl.BlockSpec((LANES, units), lambda i: (i, 0))
    return pl.pallas_call(
        run,
        name="place_mlp",
        grid=(width // LANES,),
        in_specs=[pl.BlockSpec((LANES, 3 * units), lambda i: (i, 0))],
        out_specs=[block, block, pl.BlockSpec((units, LANES), lambda i: (0, i))],
        out_shape=[sds((width, units)), sds((width, units)), sds((units, width))],
        cost_estimate=pl.CostEstimate(flops=0, bytes_accessed=18 * width * units, transcendentals=0),
        compiler_params=pltpu.CompilerParams(vmem_limit_bytes=VMEM_LIMIT),
    )(in_hbm(bundle))


def rms(features):
    return lax.rsqrt(jnp.mean(features * features, axis=-1, keepdims=True) + EPS_NORM)


def body(
    tokens,
    cotangent,
    short_lengths,
    long_lengths,
    gain_one,
    gain_two,
    w_y,
    w_x,
    conv_w,
    conv_b,
    gate_a,
    gate_x,
    bias_a,
    bias_x,
    lam,
    w_out,
    w_one,
    w_two,
    w_three,
):
    groups, rows, width = tokens.shape
    chans = w_x.shape[1]
    hidden_units = w_one.shape[1]
    total_rows = groups * rows
    ch_count, ch_index = lax.axis_size("ch"), lax.axis_index("ch")
    seq_count, seq_index = lax.axis_size("seq"), lax.axis_index("seq")
    share_rows = total_rows // ch_count
    share_width = width // ch_count
    start = (seq_index * rows).astype(jnp.int32)[None]
    grouped = lambda a: a.reshape(groups, rows, a.shape[-1])
    mine = lambda a: lax.dynamic_slice_in_dim(a, ch_index * share_rows, share_rows, 0)

    tokens = tokens.reshape(total_rows, width)
    cotangent = cotangent.reshape(total_rows, width)
    tokens_f = tokens.astype(F32)
    tokens_share = mine(tokens)
    scale_one = rms(tokens_f)
    normed_one = (tokens_f * scale_one * gain_one).astype(BF16)
    conv_input = grouped(dot(normed_one, w_x, ((1,), (0,))).astype(BF16))
    edge = shifted(conv_input[:, rows - TAPS + 1 :], "seq", 1)
    gate_pre = grouped(dot(normed_one, w_y, ((1,), (0,))))

    decay = (-8.0 * jax.nn.softplus(-lam))[None]
    lam_slope = (8.0 * jax.nn.sigmoid(-lam))[None]
    big = sds((groups, rows, chans))
    flops = 2 * total_rows * chans * chans
    conv_out, rate, inlet, keep, decay_run, local_state, carry = run_kernel(
        forward_kernel,
        "conv_gates_scan",
        [big] * 6 + [sds((2, groups, chans))],
        [
            start,
            short_lengths,
            long_lengths,
            conv_input,
            edge,
            conv_w,
            conv_b[None],
            gate_a,
            gate_x,
            bias_a[None],
            bias_x[None],
            decay,
        ],
        [pltpu.VMEM((groups, HALO + rows, chans), F32)],
        flops=2 * flops,
        smem=3,
    )
    state_in = carried_in(carry, False)
    hidden = local_state + decay_run * state_in[:, None]
    mixed_in = (hidden * jax.nn.gelu(gate_pre, approximate=True)).astype(BF16)
    mixed_in = mixed_in.reshape(total_rows, chans)
    share = sds((share_rows, width))
    to_all = sds((ch_count, share_rows, width), BF16)
    resid_share, normed_two = run_kernel(
        mid_kernel,
        "resid_mid_norm",
        [share, to_all],
        [exchange(by_owner(dot(mixed_in, w_out, ((1,), (0,))))), tokens_share, gain_two[None]],
        waits=20,
    )
    normed_two = exchange(normed_two).reshape(total_rows, width)

    d_hidden = dot(cotangent, w_three, ((1,), (1,)))
    two_parts, mlp_hidden, g_mlp = mlp_back(normed_two, d_hidden, w_one, w_two, cotangent, ch_count)
    partial_out = lax.optimization_barrier(by_owner(dot(mlp_hidden, w_three, ((1,), (0,)))))
    d_mid, gain_two_part, d_mix = run_kernel(
        mid_back_kernel,
        "d_mid",
        [share, sds((1, width)), to_all],
        [exchange(two_parts), resid_share, mine(cotangent), gain_two[None]],
        after=[g_mlp, partial_out],
        waits=20,
    )
    d_mix = exchange(d_mix).reshape(total_rows, width)
    g_mlp = lax.psum_scatter(g_mlp, "seq", scatter_dimension=0, tiled=True)

    d_mixed = grouped(dot(d_mix, w_out, ((1,), (1,))))
    d_gate_pre, reach, local_adjoint, carry_back = run_kernel(
        adjoint_kernel,
        "adjoint_scan",
        [sds((groups, rows, chans), BF16), big, big, sds((2, groups, chans))],
        [d_mixed, gate_pre, hidden, keep],
        waits=20,
    )
    beyond = carried_in(carry_back, True)
    d_conv_head, d_input, small, g_mlp = run_kernel(
        gates_back_kernel,
        "gates_back",
        [sds((groups, TAPS - 1, chans)), big, sds((SMALL_ROWS, width))],
        [
            start,
            short_lengths,
            long_lengths,
            local_adjoint,
            reach,
            beyond,
            state_in,
            hidden,
            keep,
            rate,
            inlet,
            conv_out,
            conv_input,
            edge,
            conv_w,
            gate_a,
            gate_x,
            decay,
            lam_slope,
        ],
        [
            pltpu.VMEM((HALO + rows, chans), F32),
            pltpu.VMEM((HALO + rows, chans), F32),
            pltpu.VMEM((rows + HALO, chans), F32),
        ],
        flops=4 * flops,
        smem=3,
        passed=g_mlp,
        waits=10,
    )
    g_mlp = lax.all_gather(g_mlp, "seq", axis=0, tiled=True)
    lead = shifted(d_conv_head, "seq", -1)
    ahead = start[0] + rows + jnp.arange(TAPS - 1, dtype=jnp.int32)
    lead_masks = []
    for lengths in (short_lengths, long_lengths):
        ends = jnp.cumsum(lengths)
        doc = lambda at: jnp.sum((at[:, None] >= ends[None, :]).astype(jnp.int32), axis=1)
        lead_masks.append(jnp.stack([(doc(ahead) == doc(ahead - k)).astype(F32) for k in range(TAPS)]))
    lead_masks = jnp.stack(lead_masks)
    late = []
    for i in range(TAPS - 1):
        total = jnp.zeros((groups, chans), F32)
        for k in range(TAPS):
            j = i + k - (TAPS - 1)
            if j >= 0:
                total = total + conv_w[k] * lead_masks[:, k, j, None] * lead[:, j]
        late.append(total)
    late = jnp.pad(jnp.stack(late, axis=1), ((0, 0), (rows - TAPS + 1, 0), (0, 0)))
    d_input = (d_input + late).astype(BF16).reshape(total_rows, chans)
    d_gate_pre = d_gate_pre.reshape(total_rows, chans)

    partial_one = dot(d_input, w_x, ((1,), (1,))) + dot(d_gate_pre, w_y, ((1,), (1,)))
    gain_one_part = jnp.sum(partial_one * (tokens_f * scale_one), axis=0, keepdims=True)
    gain_parts = jnp.concatenate([gain_one_part, gain_two_part], axis=0)
    back_pieces = exchange(with_gains([by_owner(partial_one), partial_out], gain_parts))

    padded = lambda a: jnp.pad(a, ((0, 0), (0, -chans % 16)))
    d_gate_wide, mixed_wide = padded(d_gate_pre + 0.0 * d_input), padded(mixed_in + 0.0 * d_input)
    d_input_wide = padded(d_input)

    def terms(other):
        normed_half = half_of(normed_one, 1, other)
        return jnp.concatenate(
            [
                dot(d_gate_wide, normed_half, ((0,), (0,))),
                dot(mixed_wide, half_of(d_mix, 1, other), ((0,), (0,))),
                dot(d_input_wide, normed_half, ((0,), (0,))),
                half_of(small, 1, other),
            ],
            axis=0,
        )

    chunk_parts = reduce_chunk(terms(False), terms(True), 1)

    g_w_one, g_w_two, g_w_three = place_mlp(g_mlp, hidden_units)
    both, chunk = run_kernel(
        tokens_back_kernel,
        "d_tokens",
        [sds((ch_count, 2, share_rows, width), BF16), sds((chunk_parts[0].shape[0] + GAIN_ROWS, LANES), BF16)],
        [back_pieces, tokens_share, resid_share, d_mid, gain_one[None], *chunk_parts],
        after=[g_w_one],
        waits=30,
    )
    g_w_y, g_w_out, g_w_x, g_gate_a, g_gate_x, g_rows, gains = assemble(
        place_chunk,
        "place_chunk",
        lax.all_gather(chunk, "seq"),
        [
            sds((chans, width)),
            sds((chans, width)),
            sds((chans, width)),
            sds((1, chans, chans)),
            sds((1, chans, chans)),
            sds((8, 8, LANES)),
            sds((8, LANES)),
        ],
        [
            ((chans, LANES), 1),
            ((chans, LANES), 1),
            ((chans, LANES), 1),
            ((1, GATE_ROWS, chans), 1),
            ((1, GATE_ROWS, chans), 1),
            ((1, 8, LANES), 0),
            ((8, LANES), None),
        ],
        [],
    )
    g_rows = g_rows[:, 0, :chans]
    d_tokens, layer_out = split_both(exchange(both), g_w_y)
    d_tokens = d_tokens.reshape(groups, rows, width)
    layer_out = layer_out.reshape(groups, rows, width)
    return (
        layer_out,
        d_tokens,
        gains[0, :share_width],
        gains[1, :share_width],
        g_w_y.T,
        g_w_x.T,
        g_rows[4:],
        g_rows[3],
        g_gate_a,
        g_gate_x,
        g_rows[0],
        g_rows[1],
        g_rows[2],
        g_w_out,
        g_w_one,
        g_w_two,
        g_w_three,
    )


def solution(mesh):
    tokens_spec = P(None, "seq", None)
    column = P(None, "ch")
    block = P("ch", None, None)
    row = P("ch", None)
    vector = P("ch")
    return jax.shard_map(
        body,
        mesh=mesh,
        in_specs=(
            tokens_spec,
            tokens_spec,
            P(),
            P(),
            P(),
            P(),
            column,
            column,
            column,
            vector,
            block,
            block,
            vector,
            vector,
            vector,
            row,
            column,
            column,
            row,
        ),
        out_specs=(
            tokens_spec,
            tokens_spec,
            vector,
            vector,
            column,
            column,
            column,
            vector,
            block,
            block,
            vector,
            vector,
            vector,
            row,
            column,
            column,
            row,
        ),
        check_vma=False,
    )
```

```python
import math

import jax
import jax.numpy as jnp
from jax import lax
from jax.experimental import pallas as pl
from jax.experimental.pallas import tpu as pltpu
from jax.sharding import PartitionSpec as P

EPS_NORM = 1e-06
F32 = jnp.float32
BF16 = jnp.bfloat16
TAPS = 4
VMEM_LIMIT = 16 * 1024 * 1024
LANES = 256
GATE_ROWS = 24
SMALL_ROWS = 64
WIDE = 512
GAIN_ROWS = 16
HBM_PER_US = 3_600_000
HALO = 8


def dot(left, right, contract):
    return lax.dot_general(left, right, (contract, ((), ())), preferred_element_type=F32)


def expm1_neg(x):
    series = x * (
        1.0
        + x * (1 / 2)
        * (1.0 + x * (1 / 3) * (1.0 + x * (1 / 4) * (1.0 + x * (1 / 5) * (1.0 + x * (1 / 6) * (1.0 + x * (1 / 7))))))
    )
    return jnp.where(x > -0.35, series, jnp.exp(x) - 1.0)


def doc_masks(ends, count, start, rows):
    positions = start + lax.broadcasted_iota(jnp.int32, (rows, 1), 0)

    def doc(at):
        total = jnp.zeros((rows, 1), jnp.int32)
        for j in range(count):
            total = total + (at >= ends[j]).astype(jnp.int32)
        return total

    here = doc(positions)
    masks = [jnp.ones((rows, 1), F32)]
    for k in range(1, TAPS):
        same = (here == doc(positions - k)) & (positions >= k)
        masks.append(same.astype(F32))
    return masks


def row_ends(length_ref, count):
    ends, total = [], 0
    for j in range(count):
        total = total + length_ref[j]
        ends.append(total)
    return ends


def gates(ext, conv_in, edge, masks, conv_w_ref, conv_b_ref, gate_a_ref, gate_x_ref, bias_a_ref, bias_x_ref):
    rows, chans = conv_in.shape
    ext[HALO - TAPS + 1 : HALO, :] = edge.astype(F32)
    ext[HALO:, :] = conv_in.astype(F32)
    conv_out = jnp.broadcast_to(conv_b_ref[...], (rows, chans))
    for k in range(TAPS):
        conv_out = conv_out + conv_w_ref[k : k + 1, :] * ext[HALO - k : HALO - k + rows, :] * masks[k]
    low = conv_out.astype(BF16)
    rate = jax.nn.sigmoid(dot(low, gate_a_ref[0], ((1,), (0,))) + bias_a_ref[...])
    inlet = jax.nn.sigmoid(dot(low, gate_x_ref[0], ((1,), (0,))) + bias_x_ref[...])
    return conv_out, rate, inlet


def forward_kernel(
    start_ref,
    short_ref,
    long_ref,
    conv_in_ref,
    edge_ref,
    conv_w_ref,
    conv_b_ref,
    gate_a_ref,
    gate_x_ref,
    bias_a_ref,
    bias_x_ref,
    decay_ref,
    keep_ref,
    run_ref,
    state_ref,
    carry_ref,
    ext,
):
    groups, rows, chans = conv_in_ref.shape
    for g in range(groups):
        length_ref = (short_ref, long_ref)[g]
        count = length_ref.shape[0]
        masks = doc_masks(row_ends(length_ref, count), count, start_ref[0], rows)
        conv_out, rate, inlet = gates(
            ext, conv_in_ref[g], edge_ref[g], masks, conv_w_ref, conv_b_ref, gate_a_ref, gate_x_ref, bias_a_ref, bias_x_ref
        )
        log_decay = decay_ref[...] * rate
        keep_ref[g] = jnp.exp(log_decay) * masks[1]
        state_ref[g] = jnp.sqrt(-expm1_neg(2.0 * log_decay)) * inlet * conv_out

    def step(t, carried):
        out = []
        for g in range(groups):
            run, state = carried[g]
            keep = keep_ref[g, pl.ds(t, 1), :]
            run = run * keep
            state = state * keep + state_ref[g, pl.ds(t, 1), :]
            run_ref[g, pl.ds(t, 1), :] = run
            state_ref[g, pl.ds(t, 1), :] = state
            out.append((run, state))
        return tuple(out)

    first = tuple((jnp.ones((1, chans), F32), jnp.zeros((1, chans), F32)) for _ in range(groups))
    last = lax.fori_loop(0, rows, step, first, unroll=8)
    for g in range(groups):
        for j in range(carry_ref.shape[0]):
            carry_ref[j, 0, g : g + 1, :] = last[g][0]
            carry_ref[j, 1, g : g + 1, :] = last[g][1]


def gelu_parts(x):
    root = 0.7978845608028654
    cubic = 0.044715
    inner = root * (x + cubic * x * x * x)
    th = jnp.tanh(inner)
    half = 0.5 * (1.0 + th)
    slope = half + 0.5 * x * (1.0 - th * th) * root * (1.0 + 3.0 * cubic * x * x)
    return x * half, slope


def adjoint_kernel(
    d_mixed_ref,
    gate_pre_ref,
    hidden_ref,
    keep_ref,
    d_gate_pre_ref,
    reach_ref,
    adj_ref,
    carry_ref,
):
    groups, rows, chans = d_mixed_ref.shape
    for g in range(groups):
        branch, slope = gelu_parts(gate_pre_ref[g])
        d_mixed = d_mixed_ref[g]
        d_gate_pre_ref[g] = (d_mixed * hidden_ref[g] * slope).astype(BF16)
        adj_ref[g] = d_mixed * branch

    def step(i, carried):
        t = rows - 1 - i
        out = []
        for g in range(groups):
            reach, passed = carried[g]
            adj = adj_ref[g, pl.ds(t, 1), :] + passed
            adj_ref[g, pl.ds(t, 1), :] = adj
            reach_ref[g, pl.ds(t, 1), :] = reach
            keep = keep_ref[g, pl.ds(t, 1), :]
            out.append((reach * keep, adj * keep))
        return tuple(out)

    first = tuple((jnp.ones((1, chans), F32), jnp.zeros((1, chans), F32)) for _ in range(groups))
    last = lax.fori_loop(0, rows, step, first, unroll=8)
    for g in range(groups):
        for j in range(carry_ref.shape[0]):
            carry_ref[j, 0, g : g + 1, :] = last[g][0]
            carry_ref[j, 1, g : g + 1, :] = last[g][1]


def gates_back_kernel(
    midway,
    start_ref,
    short_ref,
    long_ref,
    adj_ref,
    reach_ref,
    beyond_ref,
    state_in_ref,
    hidden_ref,
    keep_ref,
    conv_in_ref,
    edge_ref,
    conv_w_ref,
    conv_b_ref,
    gate_a_ref,
    gate_x_ref,
    bias_a_ref,
    bias_x_ref,
    decay_ref,
    lam_slope_ref,
    d_conv_head_ref,
    d_input_ref,
    small_ref,
    ext,
    prior,
    d_ext,
):
    groups, rows, chans = adj_ref.shape
    sums = [jnp.zeros((1, chans), F32) for _ in range(8)]
    grad_a = grad_x = jnp.zeros((chans, chans), F32)
    for g in range(groups):
        length_ref = (short_ref, long_ref)[g]
        count = length_ref.shape[0]
        ends = row_ends(length_ref, count)
        masks = doc_masks(ends, count, start_ref[0], rows)
        adjoint = adj_ref[g] + reach_ref[g] * beyond_ref[g : g + 1, :]
        prior[HALO - 1 : HALO, :] = state_in_ref[g : g + 1, :]
        prior[HALO:, :] = hidden_ref[g]
        d_keep = adjoint * prior[HALO - 1 : HALO - 1 + rows, :]
        conv_out, rate, inlet = gates(
            ext, conv_in_ref[g], edge_ref[g], masks, conv_w_ref, conv_b_ref, gate_a_ref, gate_x_ref, bias_a_ref, bias_x_ref
        )
        decay = decay_ref[...]
        log_decay = decay * rate
        square = -expm1_neg(2.0 * log_decay)
        root = jnp.sqrt(square)
        driven = adjoint * conv_out
        d_log = d_keep * keep_ref[g] - driven * inlet * (1.0 - square) / root
        d_rate_pre = d_log * decay * rate * (1.0 - rate)
        d_inlet_pre = driven * root * inlet * (1.0 - inlet)
        sums[0] = sums[0] + jnp.sum(d_rate_pre, axis=0, keepdims=True)
        sums[1] = sums[1] + jnp.sum(d_inlet_pre, axis=0, keepdims=True)
        sums[2] = sums[2] + jnp.sum(d_log * rate, axis=0, keepdims=True)
        low = conv_out.astype(BF16)
        low_a = d_rate_pre.astype(BF16)
        low_x = d_inlet_pre.astype(BF16)
        grad_a = grad_a + dot(low, low_a, ((0,), (0,)))
        grad_x = grad_x + dot(low, low_x, ((0,), (0,)))
        d_conv = (
            adjoint * root * inlet
            + dot(low_a, gate_a_ref[0], ((1,), (1,)))
            + dot(low_x, gate_x_ref[0], ((1,), (1,)))
        )
        sums[3] = sums[3] + jnp.sum(d_conv, axis=0, keepdims=True)
        d_input = conv_w_ref[0:1, :] * d_conv
        sums[4] = sums[4] + jnp.sum(d_conv * ext[HALO:, :], axis=0, keepdims=True)
        d_ext[rows:, :] = jnp.zeros((HALO, chans), F32)
        for k in range(1, TAPS):
            masked = d_conv * masks[k]
            sums[4 + k] = sums[4 + k] + jnp.sum(
                masked * ext[HALO - k : HALO - k + rows, :], axis=0, keepdims=True
            )
            d_ext[:rows, :] = masked
            d_input = d_input + conv_w_ref[k : k + 1, :] * d_ext[k : k + rows, :]
        d_input_ref[g] = d_input
        d_conv_head_ref[g] = d_conv[: TAPS - 1, :]
        if g == 0:
            midway()
    sums[2] = sums[2] * lam_slope_ref[...]
    small_ref[...] = jnp.zeros(small_ref.shape, F32)
    for i, total in enumerate(sums):
        lanes = slice(LANES * i, LANES * i + chans)
        first, last = GATE_ROWS * i, min(GATE_ROWS * (i + 1), chans)
        small_ref[: last - first, lanes] = grad_a[first:last]
        small_ref[GATE_ROWS : GATE_ROWS + last - first, lanes] = grad_x[first:last]
        small_ref[2 * GATE_ROWS : 2 * GATE_ROWS + 1, lanes] = total


def sds(shape, dtype=F32):
    return jax.ShapeDtypeStruct(shape, dtype)


def in_hbm(array):
    return pltpu.with_memory_space_constraint(array, pltpu.HBM)


class Late:
    def __init__(self, array):
        self.array = in_hbm(array)


class Arriving:
    def __init__(self, copy, ref):
        self.copy, self.ref, self.shape = copy, ref, ref.shape
        copy.start()

    def wait(self):
        if self.copy is not None:
            self.copy.wait()
            self.copy = None

    def __getitem__(self, index):
        self.wait()
        return self.ref[index]


def run_kernel(kernel, name, outs, ins, scratch=(), flops=0, smem=0, after=(), passed=None, waits=0):
    vmem = pl.BlockSpec(memory_space=pltpu.VMEM)
    scalar = pl.BlockSpec(memory_space=pltpu.SMEM)
    anywhere = pl.BlockSpec(memory_space=pl.ANY)
    late = [isinstance(a, Late) for a in ins]
    ins = [a.array if isinstance(a, Late) else a for a in ins]
    moved = sum(a.size * a.dtype.itemsize for a in list(ins) + list(outs))
    count, skip = len(ins), len(after)
    in_specs = [scalar] * smem + [anywhere if l else vmem for l in late[smem:]] + [anywhere] * skip
    held = [pltpu.VMEM(a.shape, a.dtype) for a, l in zip(ins, late) if l]
    ins = [*ins, *[in_hbm(a) for a in after]]
    out_specs = [vmem] * len(outs)
    outs, scratch = list(outs), list(scratch)
    if passed is not None:
        ins.append(in_hbm(passed))
        in_specs.append(anywhere)
        outs.append(pltpu.HBM(passed.shape, passed.dtype))
        out_specs.append(anywhere)
        scratch += [pltpu.VMEM(passed.shape, passed.dtype), pltpu.SemaphoreType.DMA((2,))]

    def run(*refs):
        if held:
            refs, arrived, sems = list(refs[: -len(held) - 1]), refs[-len(held) - 1 : -1], refs[-1]
            for n, i in enumerate([i for i in range(count) if late[i]]):
                refs[i] = Arriving(pltpu.make_async_copy(refs[i], arrived[n], sems.at[n]), arrived[n])
        if passed is None:
            kernel(*refs[:count], *refs[count + skip :])
            for ref in refs[:count]:
                if isinstance(ref, Arriving):
                    ref.wait()
            return
        in_ref, out_ref = refs[count + skip], refs[count + skip + len(outs)]
        buffer, both_sems = refs[-2:]
        fetch = pltpu.make_async_copy(in_ref, buffer, both_sems.at[0])
        store = pltpu.make_async_copy(buffer, out_ref, both_sems.at[1])
        fetch.start()

        def midway():
            fetch.wait()
            store.start()

        kept = refs[count + skip + 1 : count + skip + len(outs)]
        kernel(midway, *refs[:count], *kept, *refs[count + skip + len(outs) + 1 : -2])
        store.wait()

    return pl.pallas_call(
        run,
        name=name,
        out_shape=outs,
        in_specs=in_specs,
        out_specs=out_specs,
        scratch_shapes=scratch + ([*held, pltpu.SemaphoreType.DMA((len(held),))] if held else []),
        cost_estimate=pl.CostEstimate(flops=flops, bytes_accessed=moved + waits * HBM_PER_US, transcendentals=0),
        compiler_params=pltpu.CompilerParams(vmem_limit_bytes=VMEM_LIMIT),
    )(*ins)


def front(tokens, gain, w_x, w_y, groups):
    total, width = tokens.shape
    chans = w_x.shape[0]
    rows = total // groups
    step = total // 4

    def run(gain_ref, *refs):
        sources, outs, held, kept, sems = refs[:3], refs[3:8], refs[8:10], refs[10:13], refs[13]
        normed_out, scale_ref, conv_in_ref, edge_ref, gate_out = outs
        tokens_ref, normed_ref, gate_ref = kept
        reads = []
        for n in range(4):
            part = pl.ds(n * step, step)
            reads.append(pltpu.make_async_copy(sources[0].at[part], tokens_ref.at[part], sems.at[n]))
            reads[-1].start()
        w_x_ref, w_y_ref = [
            Arriving(pltpu.make_async_copy(source, ref, sems.at[4 + n]), ref)
            for n, (source, ref) in enumerate(zip(sources[1:], held))
        ]
        stores = []
        for n in range(4):
            reads[n].wait()
            for at in range(n * step, (n + 1) * step, 32):
                part = slice(at, at + 32)
                features = tokens_ref[part, :].astype(F32)
                scale = rms(features)
                scale_ref[part, :] = scale
                normed_ref[part, :] = (features * scale * gain_ref[...]).astype(BF16)
            part = pl.ds(n * step, step)
            stores.append(pltpu.make_async_copy(normed_ref.at[part], normed_out.at[part], sems.at[6 + n]))
            stores[-1].start()
        for g in range(groups):
            part = normed_ref[g * rows : (g + 1) * rows, :]
            gate_ref[g] = dot(part, w_y_ref[...], ((1,), (1,)))
        stores.append(pltpu.make_async_copy(gate_ref, gate_out, sems.at[10]))
        stores[-1].start()
        for g in range(groups):
            part = normed_ref[g * rows : (g + 1) * rows, :]
            conv_in = dot(part, w_x_ref[...], ((1,), (1,))).astype(BF16)
            conv_in_ref[g] = conv_in
            edge_ref[g] = conv_in[rows - TAPS + 1 :, :]
        for store in stores:
            store.wait()

    vmem = pl.BlockSpec(memory_space=pltpu.VMEM)
    anywhere = pl.BlockSpec(memory_space=pl.ANY)
    return pl.pallas_call(
        run,
        name="front",
        in_specs=[vmem] + [anywhere] * 3,
        out_specs=[anywhere, vmem, vmem, vmem, anywhere],
        out_shape=[
            pltpu.HBM((total, width), BF16),
            sds((total, 1)),
            sds((groups, rows, chans), BF16),
            sds((groups, TAPS - 1, chans), BF16),
            pltpu.HBM((groups, rows, chans), F32),
        ],
        scratch_shapes=[
            pltpu.VMEM(w_x.shape, BF16),
            pltpu.VMEM(w_y.shape, BF16),
            pltpu.VMEM((total, width), BF16),
            pltpu.VMEM((total, width), BF16),
            pltpu.VMEM((groups, rows, chans), F32),
            pltpu.SemaphoreType.DMA((11,)),
        ],
        cost_estimate=pl.CostEstimate(
            flops=4 * total * chans * width, bytes_accessed=4 * total * width, transcendentals=0
        ),
        compiler_params=pltpu.CompilerParams(vmem_limit_bytes=VMEM_LIMIT),
    )(gain[None], in_hbm(tokens), in_hbm(w_x), in_hbm(w_y))


def shifted(block, axis, distance):
    count = lax.axis_size(axis)
    route = [(i - distance, i) for i in range(count) if 0 <= i - distance < count]
    return lax.ppermute(block, axis, route)


def carried_in(value, backward):
    count, mine = lax.axis_size("seq"), lax.axis_index("seq")
    pieces = lax.all_to_all(value, "seq", 0, 0)
    total = jnp.zeros(value.shape[2:], F32)
    for j in range(count - 1, 0, -1) if backward else range(count - 1):
        longer = pieces[j, 1] + pieces[j, 0] * total
        total = jnp.where((j > mine) if backward else (j < mine), longer, total)
    return total


def sum_parts(got_ref):
    total = got_ref[0].astype(F32)
    for j in range(1, got_ref.shape[0]):
        total = total + got_ref[j].astype(F32)
    return total


def send_to_all(out_ref, share):
    share = share.astype(BF16)
    for j in range(out_ref.shape[0]):
        out_ref[j] = share


def norm_back(features, gain, grad):
    scale = rms(features)
    gained = gain * grad
    mean = jnp.mean(gained * features, axis=-1, keepdims=True)
    back = scale * gained - features * (scale * scale * scale) * mean
    return back, jnp.sum(grad * (features * scale), axis=0, keepdims=True)


def mid_kernel(got_ref, tokens_ref, gain_ref, resid_ref, normed_ref):
    resid = tokens_ref[...].astype(F32) + sum_parts(got_ref)
    resid_ref[...] = resid
    send_to_all(normed_ref, resid * rms(resid) * gain_ref[...])


def mid_back_kernel(got_ref, resid_ref, cotangent_ref, gain_ref, d_mid_ref, g_gain_ref, d_mix_ref):
    back, g_gain = norm_back(resid_ref[...], gain_ref[...], sum_parts(got_ref))
    d_mid = cotangent_ref[...].astype(F32) + back
    d_mid_ref[...] = d_mid
    g_gain_ref[...] = g_gain
    send_to_all(d_mix_ref, d_mid)


def tokens_back_kernel(got_ref, tokens_ref, resid_ref, d_mid_ref, gain_ref, *refs):
    *chunk_refs, both_ref, sent_ref = refs
    width = tokens_ref.shape[1]
    total = sum_parts(got_ref)
    rows, lanes = chunk_refs[0].shape
    chunk = chunk_refs[0][...].astype(F32)
    for chunk_ref in chunk_refs[1:]:
        chunk = chunk + chunk_ref[...].astype(F32)
    gains = total[:GAIN_ROWS, 2 * width :]
    sent_ref[:rows, :] = chunk.astype(BF16)
    sent_ref[rows:, : gains.shape[1]] = gains.astype(BF16)
    sent_ref[rows:, gains.shape[1] :] = jnp.zeros((GAIN_ROWS, lanes - gains.shape[1]), BF16)
    back, _ = norm_back(tokens_ref[...].astype(F32), gain_ref[...], total[:, :width])
    d_tokens = (d_mid_ref[...] + back).astype(BF16)
    layer_out = (resid_ref[...] + total[:, width : 2 * width]).astype(BF16)
    for j in range(both_ref.shape[0]):
        both_ref[j, 0] = d_tokens
        both_ref[j, 1] = layer_out


def split_both(both, after):
    owners, _, share, width = both.shape
    parts = 8
    step = owners // parts

    def run(both_hbm, after_ref, d_tokens_hbm, layer_hbm, held, wide, sems):
        reads, stores = [], []
        for n in range(parts):
            part = pl.ds(n * step, step)
            reads.append(pltpu.make_async_copy(both_hbm.at[part], held.at[part], sems.at[n]))
            reads[-1].start()
        for n in range(parts):
            part = pl.ds(n * step, step)
            reads[n].wait()
            stores.append(pltpu.make_async_copy(held.at[part, 1], layer_hbm.at[part], sems.at[parts + n]))
            stores[-1].start()
            wide[n * step : (n + 1) * step] = held[n * step : (n + 1) * step, 0].astype(F32)
            stores.append(pltpu.make_async_copy(wide.at[part], d_tokens_hbm.at[part], sems.at[2 * parts + n]))
            stores[-1].start()
        for store in stores:
            store.wait()

    anywhere = pl.BlockSpec(memory_space=pl.ANY)
    return pl.pallas_call(
        run,
        name="split_both",
        in_specs=[anywhere] * 2,
        out_specs=[anywhere] * 2,
        out_shape=[pltpu.HBM((owners, share, width), F32), pltpu.HBM((owners, share, width), BF16)],
        scratch_shapes=[
            pltpu.VMEM(both.shape, BF16),
            pltpu.VMEM((owners, share, width), F32),
            pltpu.SemaphoreType.DMA((3 * parts,)),
        ],
        cost_estimate=pl.CostEstimate(flops=0, bytes_accessed=5 * both.size, transcendentals=0),
        compiler_params=pltpu.CompilerParams(vmem_limit_bytes=VMEM_LIMIT),
    )(in_hbm(both), in_hbm(after))


def exchange(pieces):
    return lax.all_to_all(pieces, "ch", 0, 0)


def by_owner(partial_sum):
    count = lax.axis_size("ch")
    rows, width = partial_sum.shape
    return partial_sum.astype(BF16).reshape(count, rows // count, width)


def with_gains(pieces, gains):
    count, share, width = pieces[0].shape
    more = gains.astype(BF16).reshape(-1, count, width // count).swapaxes(0, 1)
    more = jnp.pad(more, ((0, 0), (0, share - gains.shape[0]), (0, 0)))
    return jnp.concatenate([*pieces, more], axis=-1)


def seq_route(fn):
    count = lax.axis_size("seq")
    return [(i, fn(i) % count) for i in range(count)]


def swap_core(value):
    return lax.ppermute(value, "seq", seq_route(lambda i: i ^ 1))


def shift_z(value, hops):
    return lax.ppermute(value, "seq", seq_route(lambda i: i + 2 * hops))


def half_of(array, axis, other):
    core = lax.axis_index("seq") % 2
    size = array.shape[axis] // 2
    return lax.dynamic_slice_in_dim(array, ((1 - core) if other else core) * size, size, axis)


def reduce_chunk(kept, sent, axis):
    z = lax.axis_index("seq") // 2
    got = swap_core(sent.astype(BF16))
    size = kept.shape[axis] // 4

    def piece(hops):
        at = ((z + hops) % 4) * size
        cut = lambda a: lax.dynamic_slice_in_dim(a, at, size, axis).astype(F32)
        return (cut(kept) + cut(got)).astype(BF16)

    return [piece(0)] + [shift_z(piece(hops), hops) for hops in (1, 3, 2)]


def assemble(kernel, name, chunks, outs, specs, after):
    def out_spec(block, dim):
        return pl.BlockSpec(
            block, lambda i: tuple(i % 2 * 4 + i // 2 if d == dim else 0 for d in range(len(block)))
        )

    def run(chunks_ref, *refs):
        kernel(chunks_ref[0], *refs[len(after) :])

    return pl.pallas_call(
        run,
        name=name,
        grid=(chunks.shape[0],),
        in_specs=[pl.BlockSpec((1,) + chunks.shape[1:], lambda i: (i, 0, 0))]
        + [pl.BlockSpec(memory_space=pl.ANY)] * len(after),
        out_specs=[out_spec(*spec) for spec in specs],
        out_shape=outs,
        cost_estimate=pl.CostEstimate(
            flops=0, bytes_accessed=2 * chunks.size + sum(4 * math.prod(o.shape) for o in outs), transcendentals=0
        ),
        compiler_params=pltpu.CompilerParams(vmem_limit_bytes=VMEM_LIMIT),
    )(chunks, *[in_hbm(a) for a in after])


def place_chunk(piece, y_ref, out_ref, x_ref, gate_a_ref, gate_x_ref, rows_ref, gains_ref):
    chans = x_ref.shape[0]
    piece = piece.astype(F32)
    size = (piece.shape[0] - SMALL_ROWS - GAIN_ROWS) // 3
    y_ref[...] = piece[:chans]
    out_ref[...] = piece[size : size + chans]
    x_ref[...] = piece[2 * size : 2 * size + chans]
    at = 3 * size
    gate_a_ref[0] = piece[at : at + GATE_ROWS, :chans]
    gate_x_ref[0] = piece[at + GATE_ROWS : at + 2 * GATE_ROWS, :chans]
    rows_ref[0] = piece[at + 2 * GATE_ROWS : at + 2 * GATE_ROWS + 8]
    gains = piece[at + SMALL_ROWS : at + SMALL_ROWS + 8]

    @pl.when(pl.program_id(0) == 0)
    def _():
        gains_ref[...] = gains

    @pl.when(pl.program_id(0) > 0)
    def _():
        gains_ref[...] += gains


def mlp_back(normed, d_hidden, w_one, w_two, cotangent, owners):
    rows, width = normed.shape
    units = w_one.shape[1]
    share = rows // owners
    steps = range(0, width, WIDE)

    def run(*refs):
        ins, (parts_out, hidden_out, grads_out) = refs[:5], refs[5:8]
        held, parts, kept_hidden, grads, sems = refs[8:13], refs[13], refs[14], refs[15], refs[16]
        normed, one, two, d_hidden, cot = [
            Arriving(pltpu.make_async_copy(source, ref, sems.at[n]), ref) for n, (source, ref) in enumerate(zip(ins, held))
        ]
        stores = []

        def store(source, target):
            stores.append(pltpu.make_async_copy(source, target, sems.at[len(ins) + len(stores)]))
            stores[-1].start()

        value, slope = gelu_parts(dot(normed[...], one[...], ((1,), (0,))))
        up = dot(normed[...], two[...], ((1,), (0,)))
        hidden = (value * up).astype(BF16)
        kept_hidden[...] = hidden
        store(kept_hidden, hidden_out)
        d_gate = (d_hidden[...] * up * slope).astype(BF16)
        d_up = (d_hidden[...] * value).astype(BF16)
        for at in steps:
            cols = slice(at, at + WIDE)
            back = dot(d_gate, one[cols, :], ((1,), (1,))) + dot(d_up, two[cols, :], ((1,), (1,)))
            parts[:, :, cols] = back.astype(BF16).reshape(owners, share, WIDE)
        store(parts, parts_out)
        for at in steps:
            cols = slice(at, at + WIDE)
            grads[cols, :units] = dot(normed[:, cols], d_gate, ((0,), (0,))).astype(BF16)
            grads[cols, units : 2 * units] = dot(normed[:, cols], d_up, ((0,), (0,))).astype(BF16)
            grads[cols, 2 * units :] = dot(cot[:, cols], hidden, ((0,), (0,))).astype(BF16)
            store(grads.at[cols], grads_out.at[cols])
        for copy in stores:
            copy.wait()

    ins = [in_hbm(a) for a in (normed, w_one, w_two, d_hidden, cotangent)]
    outs = [((owners, share, width), BF16), ((rows, units), BF16), ((width, 3 * units), BF16)]
    anywhere = pl.BlockSpec(memory_space=pl.ANY)
    return pl.pallas_call(
        run,
        name="mlp",
        in_specs=[anywhere] * len(ins),
        out_specs=[anywhere] * len(outs),
        out_shape=[pltpu.HBM(*out) for out in outs],
        scratch_shapes=[pltpu.VMEM(a.shape, a.dtype) for a in ins]
        + [pltpu.VMEM(*out) for out in outs]
        + [pltpu.SemaphoreType.DMA((len(ins) + 2 + len(steps),))],
        cost_estimate=pl.CostEstimate(
            flops=14 * rows * width * units, bytes_accessed=14 * width * units, transcendentals=0
        ),
        compiler_params=pltpu.CompilerParams(vmem_limit_bytes=2 * VMEM_LIMIT),
    )(*ins)


def place_mlp(bundle, units):
    width = bundle.shape[0]

    def run(piece_ref, one_ref, two_ref, three_ref):
        one_ref[...] = piece_ref[:, :units].astype(F32)
        two_ref[...] = piece_ref[:, units : 2 * units].astype(F32)
        three_ref[...] = piece_ref[:, 2 * units :].astype(F32).T

    block = pl.BlockSpec((LANES, units), lambda i: (i, 0))
    return pl.pallas_call(
        run,
        name="place_mlp",
        grid=(width // LANES,),
        in_specs=[pl.BlockSpec((LANES, 3 * units), lambda i: (i, 0))],
        out_specs=[block, block, pl.BlockSpec((units, LANES), lambda i: (0, i))],
        out_shape=[sds((width, units)), sds((width, units)), sds((units, width))],
        cost_estimate=pl.CostEstimate(flops=0, bytes_accessed=18 * width * units, transcendentals=0),
        compiler_params=pltpu.CompilerParams(vmem_limit_bytes=VMEM_LIMIT),
    )(in_hbm(bundle))


def rms(features):
    return lax.rsqrt(jnp.mean(features * features, axis=-1, keepdims=True) + EPS_NORM)


def body(
    tokens,
    cotangent,
    short_lengths,
    long_lengths,
    gain_one,
    gain_two,
    w_y,
    w_x,
    conv_w,
    conv_b,
    gate_a,
    gate_x,
    bias_a,
    bias_x,
    lam,
    w_out,
    w_one,
    w_two,
    w_three,
):
    groups, rows, width = tokens.shape
    chans = w_x.shape[1]
    hidden_units = w_one.shape[1]
    total_rows = groups * rows
    ch_count, ch_index = lax.axis_size("ch"), lax.axis_index("ch")
    seq_count, seq_index = lax.axis_size("seq"), lax.axis_index("seq")
    share_rows = total_rows // ch_count
    share_width = width // ch_count
    start = (seq_index * rows).astype(jnp.int32)[None]
    grouped = lambda a: a.reshape(groups, rows, a.shape[-1])
    mine = lambda a: lax.dynamic_slice_in_dim(a, ch_index * share_rows, share_rows, 0)

    tokens = tokens.reshape(total_rows, width)
    cotangent = cotangent.reshape(total_rows, width)
    tokens_f = tokens.astype(F32)
    tokens_share = mine(tokens)
    normed_one, scale_one, conv_input, edge, gate_pre = front(tokens, gain_one, w_x.T, w_y.T, groups)
    edge = shifted(edge, "seq", 1)

    decay = (-8.0 * jax.nn.softplus(-lam))[None]
    lam_slope = (8.0 * jax.nn.sigmoid(-lam))[None]
    big = sds((groups, rows, chans))
    flops = 2 * total_rows * chans * chans
    keep, decay_run, local_state, carry = run_kernel(
        forward_kernel,
        "conv_gates_scan",
        [big] * 3 + [sds((seq_count, 2, groups, chans))],
        [
            start,
            short_lengths,
            long_lengths,
            conv_input,
            edge,
            conv_w,
            conv_b[None],
            gate_a,
            gate_x,
            bias_a[None],
            bias_x[None],
            decay,
        ],
        [pltpu.VMEM((HALO + rows, chans), F32)],
        flops=2 * flops,
        smem=3,
    )
    state_in = carried_in(carry, False)
    hidden = local_state + decay_run * state_in[:, None]
    mixed_in = (hidden * jax.nn.gelu(gate_pre, approximate=True)).astype(BF16)
    mixed_in = mixed_in.reshape(total_rows, chans)
    share = sds((share_rows, width))
    to_all = sds((ch_count, share_rows, width), BF16)
    resid_share, normed_two = run_kernel(
        mid_kernel,
        "resid_mid_norm",
        [share, to_all],
        [exchange(by_owner(dot(mixed_in, w_out, ((1,), (0,))))), Late(tokens_share), gain_two[None]],
        waits=20,
    )
    normed_two = exchange(normed_two).reshape(total_rows, width)

    d_hidden = dot(cotangent, w_three, ((1,), (1,)))
    two_parts, mlp_hidden, g_mlp = mlp_back(normed_two, d_hidden, w_one, w_two, cotangent, ch_count)
    partial_out = lax.optimization_barrier(by_owner(dot(mlp_hidden, w_three, ((1,), (0,)))))
    d_mid, gain_two_part, d_mix = run_kernel(
        mid_back_kernel,
        "d_mid",
        [share, sds((1, width)), to_all],
        [exchange(two_parts), Late(resid_share), Late(mine(cotangent)), gain_two[None]],
        after=[g_mlp, partial_out],
        waits=20,
    )
    d_mix = exchange(d_mix).reshape(total_rows, width)
    g_mlp = lax.psum_scatter(g_mlp, "seq", scatter_dimension=0, tiled=True)

    d_mixed = grouped(dot(d_mix, w_out, ((1,), (1,))))
    d_gate_pre, reach, local_adjoint, carry_back = run_kernel(
        adjoint_kernel,
        "adjoint_scan",
        [sds((groups, rows, chans), BF16), big, big, sds((seq_count, 2, groups, chans))],
        [d_mixed, gate_pre, hidden, keep],
        waits=20,
    )
    beyond = carried_in(carry_back, True)
    d_conv_head, d_input, small, g_mlp = run_kernel(
        gates_back_kernel,
        "gates_back",
        [sds((groups, TAPS - 1, chans)), big, sds((SMALL_ROWS, width))],
        [
            start,
            short_lengths,
            long_lengths,
            local_adjoint,
            reach,
            beyond,
            state_in,
            hidden,
            keep,
            conv_input,
            edge,
            conv_w,
            conv_b[None],
            gate_a,
            gate_x,
            bias_a[None],
            bias_x[None],
            decay,
            lam_slope,
        ],
        [
            pltpu.VMEM((HALO + rows, chans), F32),
            pltpu.VMEM((HALO + rows, chans), F32),
            pltpu.VMEM((rows + HALO, chans), F32),
        ],
        flops=4 * flops,
        smem=3,
        passed=g_mlp,
        waits=10,
    )
    g_mlp = lax.all_gather(g_mlp, "seq", axis=0, tiled=True)
    lead = shifted(d_conv_head, "seq", -1)
    ahead = start[0] + rows + jnp.arange(TAPS - 1, dtype=jnp.int32)
    lead_masks = []
    for lengths in (short_lengths, long_lengths):
        ends = jnp.cumsum(lengths)
        doc = lambda at: jnp.sum((at[:, None] >= ends[None, :]).astype(jnp.int32), axis=1)
        lead_masks.append(jnp.stack([(doc(ahead) == doc(ahead - k)).astype(F32) for k in range(TAPS)]))
    lead_masks = jnp.stack(lead_masks)
    late = []
    for i in range(TAPS - 1):
        total = jnp.zeros((groups, chans), F32)
        for k in range(TAPS):
            j = i + k - (TAPS - 1)
            if j >= 0:
                total = total + conv_w[k] * lead_masks[:, k, j, None] * lead[:, j]
        late.append(total)
    late = jnp.pad(jnp.stack(late, axis=1), ((0, 0), (rows - TAPS + 1, 0), (0, 0)))
    d_input = (d_input + late).astype(BF16).reshape(total_rows, chans)
    d_gate_pre = d_gate_pre.reshape(total_rows, chans)

    partial_one = dot(d_input, w_x, ((1,), (1,))) + dot(d_gate_pre, w_y, ((1,), (1,)))
    gain_one_part = jnp.sum(partial_one * (tokens_f * scale_one), axis=0, keepdims=True)
    gain_parts = jnp.concatenate([gain_one_part, gain_two_part], axis=0)
    back_pieces = exchange(with_gains([by_owner(partial_one), partial_out], gain_parts))

    padded = lambda a: jnp.pad(a, ((0, 0), (0, -chans % 16)))
    d_gate_wide, mixed_wide = padded(d_gate_pre + 0.0 * d_input), padded(mixed_in + 0.0 * d_input)
    d_input_wide = padded(d_input)

    def terms(other):
        normed_half = half_of(normed_one, 1, other)
        return jnp.concatenate(
            [
                dot(d_gate_wide, normed_half, ((0,), (0,))),
                dot(mixed_wide, half_of(d_mix, 1, other), ((0,), (0,))),
                dot(d_input_wide, normed_half, ((0,), (0,))),
                half_of(small, 1, other),
            ],
            axis=0,
        )

    chunk_parts = reduce_chunk(terms(False), terms(True), 1)

    g_w_one, g_w_two, g_w_three = place_mlp(g_mlp, hidden_units)
    both, chunk = run_kernel(
        tokens_back_kernel,
        "d_tokens",
        [sds((ch_count, 2, share_rows, width), BF16), sds((chunk_parts[0].shape[0] + GAIN_ROWS, LANES), BF16)],
        [back_pieces, Late(tokens_share), Late(resid_share), Late(d_mid), gain_one[None], *chunk_parts],
        after=[g_w_one],
        waits=30,
    )
    g_w_y, g_w_out, g_w_x, g_gate_a, g_gate_x, g_rows, gains = assemble(
        place_chunk,
        "place_chunk",
        lax.all_gather(chunk, "seq"),
        [
            sds((chans, width)),
            sds((chans, width)),
            sds((chans, width)),
            sds((1, chans, chans)),
            sds((1, chans, chans)),
            sds((8, 8, LANES)),
            sds((8, LANES)),
        ],
        [
            ((chans, LANES), 1),
            ((chans, LANES), 1),
            ((chans, LANES), 1),
            ((1, GATE_ROWS, chans), 1),
            ((1, GATE_ROWS, chans), 1),
            ((1, 8, LANES), 0),
            ((8, LANES), None),
        ],
        [],
    )
    g_rows = g_rows[:, 0, :chans]
    d_tokens, layer_out = split_both(exchange(both), g_w_y)
    d_tokens = d_tokens.reshape(groups, rows, width)
    layer_out = layer_out.reshape(groups, rows, width)
    return (
        layer_out,
        d_tokens,
        gains[0, :share_width],
        gains[1, :share_width],
        g_w_y.T,
        g_w_x.T,
        g_rows[4:],
        g_rows[3],
        g_gate_a,
        g_gate_x,
        g_rows[0],
        g_rows[1],
        g_rows[2],
        g_w_out,
        g_w_one,
        g_w_two,
        g_w_three,
    )


def solution(mesh):
    tokens_spec = P(None, "seq", None)
    column = P(None, "ch")
    block = P("ch", None, None)
    row = P("ch", None)
    vector = P("ch")
    return jax.shard_map(
        body,
        mesh=mesh,
        in_specs=(
            tokens_spec,
            tokens_spec,
            P(),
            P(),
            P(),
            P(),
            column,
            column,
            column,
            vector,
            block,
            block,
            vector,
            vector,
            vector,
            row,
            column,
            column,
            row,
        ),
        out_specs=(
            tokens_spec,
            tokens_spec,
            vector,
            vector,
            column,
            column,
            column,
            vector,
            block,
            block,
            vector,
            vector,
            vector,
            row,
            column,
            column,
            row,
        ),
        check_vma=False,
    )
```

```python
import math

import jax
import jax.numpy as jnp
from jax import lax
from jax.experimental import pallas as pl
from jax.experimental.pallas import tpu as pltpu
from jax.sharding import PartitionSpec as P

EPS_NORM = 1e-06
F32 = jnp.float32
BF16 = jnp.bfloat16
TAPS = 4
VMEM_LIMIT = 16 * 1024 * 1024
LANES = 256
GATE_ROWS = 24
SMALL_ROWS = 64
WIDE = 512
GAIN_ROWS = 16
HBM_PER_US = 3_600_000
HALO = 8


def dot(left, right, contract):
    return lax.dot_general(left, right, (contract, ((), ())), preferred_element_type=F32)


def expm1_neg(x):
    series = x * (
        1.0
        + x * (1 / 2)
        * (1.0 + x * (1 / 3) * (1.0 + x * (1 / 4) * (1.0 + x * (1 / 5) * (1.0 + x * (1 / 6) * (1.0 + x * (1 / 7))))))
    )
    return jnp.where(x > -0.35, series, jnp.exp(x) - 1.0)


def doc_masks(ends, count, start, rows):
    positions = start + lax.broadcasted_iota(jnp.int32, (rows, 1), 0)

    def doc(at):
        total = jnp.zeros((rows, 1), jnp.int32)
        for j in range(count):
            total = total + (at >= ends[j]).astype(jnp.int32)
        return total

    here = doc(positions)
    masks = [jnp.ones((rows, 1), F32)]
    for k in range(1, TAPS):
        same = (here == doc(positions - k)) & (positions >= k)
        masks.append(same.astype(F32))
    return masks


def row_ends(length_ref, count):
    ends, total = [], 0
    for j in range(count):
        total = total + length_ref[j]
        ends.append(total)
    return ends


def gates(ext, conv_in, edge, masks, conv_w_ref, conv_b_ref, gate_a_ref, gate_x_ref, bias_a_ref, bias_x_ref):
    rows, chans = conv_in.shape
    ext[HALO - TAPS + 1 : HALO, :] = edge.astype(F32)
    ext[HALO:, :] = conv_in.astype(F32)
    conv_out = jnp.broadcast_to(conv_b_ref[...], (rows, chans))
    for k in range(TAPS):
        conv_out = conv_out + conv_w_ref[k : k + 1, :] * ext[HALO - k : HALO - k + rows, :] * masks[k]
    low = conv_out.astype(BF16)
    rate = jax.nn.sigmoid(dot(low, gate_a_ref[0], ((1,), (0,))) + bias_a_ref[...])
    inlet = jax.nn.sigmoid(dot(low, gate_x_ref[0], ((1,), (0,))) + bias_x_ref[...])
    return conv_out, rate, inlet


def forward_kernel(
    start_ref,
    short_ref,
    long_ref,
    conv_in_ref,
    edge_ref,
    conv_w_ref,
    conv_b_ref,
    gate_a_ref,
    gate_x_ref,
    bias_a_ref,
    bias_x_ref,
    decay_ref,
    keep_ref,
    run_ref,
    state_ref,
    carry_ref,
    ext,
):
    groups, rows, chans = conv_in_ref.shape
    for g in range(groups):
        length_ref = (short_ref, long_ref)[g]
        count = length_ref.shape[0]
        masks = doc_masks(row_ends(length_ref, count), count, start_ref[0], rows)
        conv_out, rate, inlet = gates(
            ext, conv_in_ref[g], edge_ref[g], masks, conv_w_ref, conv_b_ref, gate_a_ref, gate_x_ref, bias_a_ref, bias_x_ref
        )
        log_decay = decay_ref[...] * rate
        keep_ref[g] = jnp.exp(log_decay) * masks[1]
        state_ref[g] = jnp.sqrt(-expm1_neg(2.0 * log_decay)) * inlet * conv_out

    def step(t, carried):
        out = []
        for g in range(groups):
            run, state = carried[g]
            keep = keep_ref[g, pl.ds(t, 1), :]
            run = run * keep
            state = state * keep + state_ref[g, pl.ds(t, 1), :]
            run_ref[g, pl.ds(t, 1), :] = run
            state_ref[g, pl.ds(t, 1), :] = state
            out.append((run, state))
        return tuple(out)

    first = tuple((jnp.ones((1, chans), F32), jnp.zeros((1, chans), F32)) for _ in range(groups))
    last = lax.fori_loop(0, rows, step, first, unroll=8)
    for g in range(groups):
        for j in range(carry_ref.shape[0]):
            carry_ref[j, 0, g : g + 1, :] = last[g][0]
            carry_ref[j, 1, g : g + 1, :] = last[g][1]


def gelu_parts(x):
    root = 0.7978845608028654
    cubic = 0.044715
    inner = root * (x + cubic * x * x * x)
    th = jnp.tanh(inner)
    half = 0.5 * (1.0 + th)
    slope = half + 0.5 * x * (1.0 - th * th) * root * (1.0 + 3.0 * cubic * x * x)
    return x * half, slope


def adjoint_kernel(
    d_mixed_ref,
    gate_pre_ref,
    hidden_ref,
    keep_ref,
    d_gate_pre_ref,
    reach_ref,
    adj_ref,
    carry_ref,
):
    groups, rows, chans = d_mixed_ref.shape
    for g in range(groups):
        branch, slope = gelu_parts(gate_pre_ref[g])
        d_mixed = d_mixed_ref[g]
        d_gate_pre_ref[g] = (d_mixed * hidden_ref[g] * slope).astype(BF16)
        adj_ref[g] = d_mixed * branch

    def step(i, carried):
        t = rows - 1 - i
        out = []
        for g in range(groups):
            reach, passed = carried[g]
            adj = adj_ref[g, pl.ds(t, 1), :] + passed
            adj_ref[g, pl.ds(t, 1), :] = adj
            reach_ref[g, pl.ds(t, 1), :] = reach
            keep = keep_ref[g, pl.ds(t, 1), :]
            out.append((reach * keep, adj * keep))
        return tuple(out)

    first = tuple((jnp.ones((1, chans), F32), jnp.zeros((1, chans), F32)) for _ in range(groups))
    last = lax.fori_loop(0, rows, step, first, unroll=8)
    for g in range(groups):
        for j in range(carry_ref.shape[0]):
            carry_ref[j, 0, g : g + 1, :] = last[g][0]
            carry_ref[j, 1, g : g + 1, :] = last[g][1]


def gates_back_kernel(
    midway,
    start_ref,
    short_ref,
    long_ref,
    adj_ref,
    reach_ref,
    beyond_ref,
    state_in_ref,
    hidden_ref,
    keep_ref,
    conv_in_ref,
    edge_ref,
    conv_w_ref,
    conv_b_ref,
    gate_a_ref,
    gate_x_ref,
    bias_a_ref,
    bias_x_ref,
    decay_ref,
    lam_slope_ref,
    d_conv_head_ref,
    d_input_ref,
    small_ref,
    ext,
    prior,
    d_ext,
):
    groups, rows, chans = adj_ref.shape
    sums = [jnp.zeros((1, chans), F32) for _ in range(8)]
    grad_a = grad_x = jnp.zeros((chans, chans), F32)
    for g in range(groups):
        length_ref = (short_ref, long_ref)[g]
        count = length_ref.shape[0]
        ends = row_ends(length_ref, count)
        masks = doc_masks(ends, count, start_ref[0], rows)
        adjoint = adj_ref[g] + reach_ref[g] * beyond_ref[g : g + 1, :]
        prior[HALO - 1 : HALO, :] = state_in_ref[g : g + 1, :]
        prior[HALO:, :] = hidden_ref[g]
        d_keep = adjoint * prior[HALO - 1 : HALO - 1 + rows, :]
        conv_out, rate, inlet = gates(
            ext, conv_in_ref[g], edge_ref[g], masks, conv_w_ref, conv_b_ref, gate_a_ref, gate_x_ref, bias_a_ref, bias_x_ref
        )
        decay = decay_ref[...]
        log_decay = decay * rate
        square = -expm1_neg(2.0 * log_decay)
        root = jnp.sqrt(square)
        driven = adjoint * conv_out
        d_log = d_keep * keep_ref[g] - driven * inlet * (1.0 - square) / root
        d_rate_pre = d_log * decay * rate * (1.0 - rate)
        d_inlet_pre = driven * root * inlet * (1.0 - inlet)
        sums[0] = sums[0] + jnp.sum(d_rate_pre, axis=0, keepdims=True)
        sums[1] = sums[1] + jnp.sum(d_inlet_pre, axis=0, keepdims=True)
        sums[2] = sums[2] + jnp.sum(d_log * rate, axis=0, keepdims=True)
        low = conv_out.astype(BF16)
        low_a = d_rate_pre.astype(BF16)
        low_x = d_inlet_pre.astype(BF16)
        grad_a = grad_a + dot(low, low_a, ((0,), (0,)))
        grad_x = grad_x + dot(low, low_x, ((0,), (0,)))
        d_conv = (
            adjoint * root * inlet
            + dot(low_a, gate_a_ref[0], ((1,), (1,)))
            + dot(low_x, gate_x_ref[0], ((1,), (1,)))
        )
        sums[3] = sums[3] + jnp.sum(d_conv, axis=0, keepdims=True)
        d_input = conv_w_ref[0:1, :] * d_conv
        sums[4] = sums[4] + jnp.sum(d_conv * ext[HALO:, :], axis=0, keepdims=True)
        d_ext[rows:, :] = jnp.zeros((HALO, chans), F32)
        for k in range(1, TAPS):
            masked = d_conv * masks[k]
            sums[4 + k] = sums[4 + k] + jnp.sum(
                masked * ext[HALO - k : HALO - k + rows, :], axis=0, keepdims=True
            )
            d_ext[:rows, :] = masked
            d_input = d_input + conv_w_ref[k : k + 1, :] * d_ext[k : k + rows, :]
        d_input_ref[g] = d_input
        d_conv_head_ref[g] = d_conv[: TAPS - 1, :]
        if g == 0:
            midway()
    sums[2] = sums[2] * lam_slope_ref[...]
    small_ref[...] = jnp.zeros(small_ref.shape, F32)
    for i, total in enumerate(sums):
        lanes = slice(LANES * i, LANES * i + chans)
        first, last = GATE_ROWS * i, min(GATE_ROWS * (i + 1), chans)
        small_ref[: last - first, lanes] = grad_a[first:last]
        small_ref[GATE_ROWS : GATE_ROWS + last - first, lanes] = grad_x[first:last]
        small_ref[2 * GATE_ROWS : 2 * GATE_ROWS + 1, lanes] = total


def sds(shape, dtype=F32):
    return jax.ShapeDtypeStruct(shape, dtype)


def in_hbm(array):
    return pltpu.with_memory_space_constraint(array, pltpu.HBM)


class Late:
    def __init__(self, array, share=0):
        self.array, self.share = in_hbm(array), share
        self.held = pltpu.VMEM((share or array.shape[0],) + array.shape[1:], array.dtype)

    def source(self, ref):
        if not self.share:
            return ref
        at = pl.multiple_of(lax.axis_index("ch") * self.share, self.share)
        return ref.at[pl.ds(at, self.share)]


class Arriving:
    def __init__(self, copy, ref):
        self.copy, self.ref, self.shape = copy, ref, ref.shape
        copy.start()

    def wait(self):
        if self.copy is not None:
            self.copy.wait()
            self.copy = None

    def __getitem__(self, index):
        self.wait()
        return self.ref[index]


def run_kernel(kernel, name, outs, ins, scratch=(), flops=0, smem=0, after=(), passed=None, waits=0):
    vmem = pl.BlockSpec(memory_space=pltpu.VMEM)
    scalar = pl.BlockSpec(memory_space=pltpu.SMEM)
    anywhere = pl.BlockSpec(memory_space=pl.ANY)
    late = [a if isinstance(a, Late) else None for a in ins]
    ins = [a.array if isinstance(a, Late) else a for a in ins]
    moved = sum(a.size * a.dtype.itemsize for a in list(ins) + list(outs))
    count, skip = len(ins), len(after)
    in_specs = [scalar] * smem + [anywhere if l else vmem for l in late[smem:]] + [anywhere] * skip
    held = [l.held for l in late if l]
    ins = [*ins, *[in_hbm(a) for a in after]]
    out_specs = [vmem] * len(outs)
    outs, scratch = list(outs), list(scratch)
    if passed is not None:
        ins.append(in_hbm(passed))
        in_specs.append(anywhere)
        outs.append(pltpu.HBM(passed.shape, passed.dtype))
        out_specs.append(anywhere)
        scratch += [pltpu.VMEM(passed.shape, passed.dtype), pltpu.SemaphoreType.DMA((2,))]

    def run(*refs):
        if held:
            refs, arrived, sems = list(refs[: -len(held) - 1]), refs[-len(held) - 1 : -1], refs[-1]
            for n, i in enumerate([i for i in range(count) if late[i]]):
                source = late[i].source(refs[i])
                refs[i] = Arriving(pltpu.make_async_copy(source, arrived[n], sems.at[n]), arrived[n])
        if passed is None:
            kernel(*refs[:count], *refs[count + skip :])
            for ref in refs[:count]:
                if isinstance(ref, Arriving):
                    ref.wait()
            return
        in_ref, out_ref = refs[count + skip], refs[count + skip + len(outs)]
        buffer, both_sems = refs[-2:]
        fetch = pltpu.make_async_copy(in_ref, buffer, both_sems.at[0])
        store = pltpu.make_async_copy(buffer, out_ref, both_sems.at[1])
        fetch.start()

        def midway():
            fetch.wait()
            store.start()

        kept = refs[count + skip + 1 : count + skip + len(outs)]
        kernel(midway, *refs[:count], *kept, *refs[count + skip + len(outs) + 1 : -2])
        store.wait()

    return pl.pallas_call(
        run,
        name=name,
        out_shape=outs,
        in_specs=in_specs,
        out_specs=out_specs,
        scratch_shapes=scratch + ([*held, pltpu.SemaphoreType.DMA((len(held),))] if held else []),
        cost_estimate=pl.CostEstimate(flops=flops, bytes_accessed=moved + waits * HBM_PER_US, transcendentals=0),
        compiler_params=pltpu.CompilerParams(vmem_limit_bytes=VMEM_LIMIT),
    )(*ins)


def front(tokens, cotangent, gain, w_x, w_y, groups):
    total, width = tokens.shape
    share = total // lax.axis_size("ch")
    chans = w_x.shape[0]
    rows = total // groups
    step = total // 4

    def run(*refs):
        gain_hbm, sources, outs, held, kept, sems = refs[0], refs[1:5], refs[5:12], refs[12:14], refs[14:18], refs[18]
        normed_out, scale_ref, conv_in_ref, edge_ref, gate_out, tokens_share_ref, cot_share_ref = outs
        gain_ref = Arriving(pltpu.make_async_copy(gain_hbm, kept[3], sems.at[12]), kept[3])
        tokens_ref, normed_ref, gate_ref, _ = kept
        reads = []
        for n in range(4):
            part = pl.ds(n * step, step)
            reads.append(pltpu.make_async_copy(sources[0].at[part], tokens_ref.at[part], sems.at[n]))
            reads[-1].start()
        w_x_ref, w_y_ref = [
            Arriving(pltpu.make_async_copy(source, ref, sems.at[4 + n]), ref)
            for n, (source, ref) in enumerate(zip(sources[1:3], held))
        ]
        mine = pl.ds(pl.multiple_of(lax.axis_index("ch") * share, share), share)
        cot_share = pltpu.make_async_copy(sources[3].at[mine], cot_share_ref, sems.at[11])
        cot_share.start()
        stores = [cot_share]
        for n in range(4):
            reads[n].wait()
            for at in range(n * step, (n + 1) * step, 32):
                part = slice(at, at + 32)
                features = tokens_ref[part, :].astype(F32)
                scale = rms(features)
                scale_ref[part, :] = scale
                normed_ref[part, :] = (features * scale * gain_ref[...]).astype(BF16)
            part = pl.ds(n * step, step)
            stores.append(pltpu.make_async_copy(normed_ref.at[part], normed_out.at[part], sems.at[6 + n]))
            stores[-1].start()
        tokens_share_ref[...] = tokens_ref[mine, :]
        for g in range(groups):
            part = normed_ref[g * rows : (g + 1) * rows, :]
            gate_ref[g] = dot(part, w_y_ref[...], ((1,), (1,)))
        stores.append(pltpu.make_async_copy(gate_ref, gate_out, sems.at[10]))
        stores[-1].start()
        for g in range(groups):
            part = normed_ref[g * rows : (g + 1) * rows, :]
            conv_in = dot(part, w_x_ref[...], ((1,), (1,))).astype(BF16)
            conv_in_ref[g] = conv_in
            edge_ref[g] = conv_in[rows - TAPS + 1 :, :]
        for store in stores:
            store.wait()

    vmem = pl.BlockSpec(memory_space=pltpu.VMEM)
    anywhere = pl.BlockSpec(memory_space=pl.ANY)
    return pl.pallas_call(
        run,
        name="front",
        in_specs=[anywhere] * 5,
        out_specs=[anywhere, vmem, vmem, vmem, anywhere, vmem, vmem],
        out_shape=[
            pltpu.HBM((total, width), BF16),
            sds((total, 1)),
            sds((groups, rows, chans), BF16),
            sds((groups, TAPS - 1, chans), BF16),
            pltpu.HBM((groups, rows, chans), F32),
            sds((share, width), BF16),
            sds((share, width), BF16),
        ],
        scratch_shapes=[
            pltpu.VMEM(w_x.shape, BF16),
            pltpu.VMEM(w_y.shape, BF16),
            pltpu.VMEM((total, width), BF16),
            pltpu.VMEM((total, width), BF16),
            pltpu.VMEM((groups, rows, chans), F32),
            pltpu.VMEM((1, width), F32),
            pltpu.SemaphoreType.DMA((13,)),
        ],
        cost_estimate=pl.CostEstimate(
            flops=4 * total * chans * width, bytes_accessed=4 * total * width, transcendentals=0
        ),
        compiler_params=pltpu.CompilerParams(vmem_limit_bytes=VMEM_LIMIT),
    )(in_hbm(gain[None]), in_hbm(tokens), in_hbm(w_x), in_hbm(w_y), in_hbm(cotangent))


def shifted(block, axis, distance):
    count = lax.axis_size(axis)
    route = [(i - distance, i) for i in range(count) if 0 <= i - distance < count]
    return lax.ppermute(block, axis, route)


def carried_in(value, backward):
    count, mine = lax.axis_size("seq"), lax.axis_index("seq")
    pieces = lax.all_to_all(value, "seq", 0, 0)
    total = jnp.zeros(value.shape[2:], F32)
    for j in range(count - 1, 0, -1) if backward else range(count - 1):
        longer = pieces[j, 1] + pieces[j, 0] * total
        total = jnp.where((j > mine) if backward else (j < mine), longer, total)
    return total


def sum_parts(got_ref):
    total = got_ref[0].astype(F32)
    for j in range(1, got_ref.shape[0]):
        total = total + got_ref[j].astype(F32)
    return total


def send_to_all(out_ref, share):
    share = share.astype(BF16)
    for j in range(out_ref.shape[0]):
        out_ref[j] = share


def norm_back(features, gain, grad):
    scale = rms(features)
    gained = gain * grad
    mean = jnp.mean(gained * features, axis=-1, keepdims=True)
    back = scale * gained - features * (scale * scale * scale) * mean
    return back, jnp.sum(grad * (features * scale), axis=0, keepdims=True)


def mid_kernel(got_ref, tokens_ref, gain_ref, resid_ref, normed_ref):
    resid = tokens_ref[...].astype(F32) + sum_parts(got_ref)
    resid_ref[...] = resid
    send_to_all(normed_ref, resid * rms(resid) * gain_ref[...])


def mid_back_kernel(got_ref, resid_ref, cotangent_ref, gain_ref, d_mid_ref, g_gain_ref, d_mix_ref):
    back, g_gain = norm_back(resid_ref[...], gain_ref[...], sum_parts(got_ref))
    d_mid = cotangent_ref[...].astype(F32) + back
    d_mid_ref[...] = d_mid
    g_gain_ref[...] = g_gain
    send_to_all(d_mix_ref, d_mid)


def tokens_back_kernel(got_ref, tokens_ref, resid_ref, d_mid_ref, gain_ref, *refs):
    *chunk_refs, both_ref, sent_ref = refs
    width = tokens_ref.shape[1]
    total = sum_parts(got_ref)
    rows, lanes = chunk_refs[0].shape
    chunk = chunk_refs[0][...].astype(F32)
    for chunk_ref in chunk_refs[1:]:
        chunk = chunk + chunk_ref[...].astype(F32)
    gains = total[:GAIN_ROWS, 2 * width :]
    sent_ref[:rows, :] = chunk.astype(BF16)
    sent_ref[rows:, : gains.shape[1]] = gains.astype(BF16)
    sent_ref[rows:, gains.shape[1] :] = jnp.zeros((GAIN_ROWS, lanes - gains.shape[1]), BF16)
    back, _ = norm_back(tokens_ref[...].astype(F32), gain_ref[...], total[:, :width])
    d_tokens = (d_mid_ref[...] + back).astype(BF16)
    layer_out = (resid_ref[...] + total[:, width : 2 * width]).astype(BF16)
    for j in range(both_ref.shape[0]):
        both_ref[j, 0] = d_tokens
        both_ref[j, 1] = layer_out


def exchange(pieces):
    return lax.all_to_all(pieces, "ch", 0, 0)


def by_owner(partial_sum):
    count = lax.axis_size("ch")
    rows, width = partial_sum.shape
    return partial_sum.astype(BF16).reshape(count, rows // count, width)


def with_gains(pieces, gains):
    count, share, width = pieces[0].shape
    more = gains.astype(BF16).reshape(-1, count, width // count).swapaxes(0, 1)
    more = jnp.pad(more, ((0, 0), (0, share - gains.shape[0]), (0, 0)))
    return jnp.concatenate([*pieces, more], axis=-1)


def seq_route(fn):
    count = lax.axis_size("seq")
    return [(i, fn(i) % count) for i in range(count)]


def swap_core(value):
    return lax.ppermute(value, "seq", seq_route(lambda i: i ^ 1))


def shift_z(value, hops):
    return lax.ppermute(value, "seq", seq_route(lambda i: i + 2 * hops))


def half_of(array, axis, other):
    core = lax.axis_index("seq") % 2
    size = array.shape[axis] // 2
    return lax.dynamic_slice_in_dim(array, ((1 - core) if other else core) * size, size, axis)


def reduce_chunk(kept, sent, axis):
    z = lax.axis_index("seq") // 2
    got = swap_core(sent.astype(BF16))
    size = kept.shape[axis] // 4

    def piece(hops):
        at = ((z + hops) % 4) * size
        cut = lambda a: lax.dynamic_slice_in_dim(a, at, size, axis).astype(F32)
        return (cut(kept) + cut(got)).astype(BF16)

    return [piece(0)] + [shift_z(piece(hops), hops) for hops in (1, 3, 2)]


def finish(both, chunks, chans):
    owners, _, share, width = both.shape
    count = chunks.shape[0]
    wide = (chunks.shape[1] - SMALL_ROWS - GAIN_ROWS) // 3
    step = owners // 4
    gain_width = width // owners

    def run(both_ref, chunks_hbm, *refs):
        outs, kept, chunk_ref, sems = refs[:14], refs[14:27], refs[27], refs[28]
        d_tokens_hbm, layer_hbm = outs[:2]
        d_tokens_ref, y_ref, out_ref, x_ref, gate_a_ref, gate_x_ref, conv_w_ref, *rows_refs = kept
        *rows_refs, gain_one_ref, gain_two_ref = rows_refs
        reads, stores = [], []

        def store(source, target):
            stores.append(pltpu.make_async_copy(source, target, sems.at[count + len(stores)]))
            stores[-1].start()

        for i in range(count):
            reads.append(pltpu.make_async_copy(chunks_hbm.at[i], chunk_ref.at[i], sems.at[i]))
            reads[-1].start()
        store(both_ref.at[:, 1], layer_hbm)
        for n in range(4):
            part = slice(n * step, (n + 1) * step)
            d_tokens_ref[part] = both_ref[part, 0].astype(F32)
            store(d_tokens_ref.at[pl.ds(n * step, step)], d_tokens_hbm.at[pl.ds(n * step, step)])
        gains = jnp.zeros((8, LANES), F32)
        for i in range(count):
            chunk = i % 2 * 4 + i // 2
            lanes = pl.ds(chunk * LANES, LANES)
            reads[i].wait()
            for n, (ref, hbm) in enumerate(zip((y_ref, out_ref, x_ref), outs[2:5])):
                ref[:, chunk * LANES : (chunk + 1) * LANES] = chunk_ref[i, n * wide : n * wide + chans, :].astype(F32)
                store(ref.at[:, lanes], hbm.at[:, lanes])
            small = chunk_ref[i, 3 * wide :, :].astype(F32)
            for n, ref in enumerate((gate_a_ref, gate_x_ref)):
                for r in range(min(GATE_ROWS, chans - chunk * GATE_ROWS)):
                    ref[chunk * GATE_ROWS + r] = small[n * GATE_ROWS + r : n * GATE_ROWS + r + 1, :chans]
            total = small[2 * GATE_ROWS : 2 * GATE_ROWS + 1, :chans]
            if chunk < 4:
                rows_refs[chunk][...] = total
            else:
                conv_w_ref[chunk - 4 : chunk - 3, :] = total
            gains = gains + small[SMALL_ROWS : SMALL_ROWS + 8]
        gain_one_ref[...] = gains[0:1, :gain_width]
        gain_two_ref[...] = gains[1:2, :gain_width]
        for source, target in zip(kept[4:], outs[5:]):
            store(source, target)
        for copy in stores:
            copy.wait()

    weight = ((chans, width), F32)
    gate = ((chans, 1, chans), F32)
    row = ((1, chans), F32)
    gain = ((1, gain_width), F32)
    blocks = ((owners, share, width), F32)
    small = [gate, gate, ((TAPS, chans), F32), row, row, row, row, gain, gain]
    anywhere = pl.BlockSpec(memory_space=pl.ANY)
    return pl.pallas_call(
        run,
        name="finish",
        in_specs=[pl.BlockSpec(memory_space=pltpu.VMEM), anywhere],
        out_specs=[anywhere] * 14,
        out_shape=[pltpu.HBM(*out) for out in (blocks, (blocks[0], BF16), weight, weight, weight, *small)],
        scratch_shapes=[pltpu.VMEM(*out) for out in (blocks, weight, weight, weight, *small)]
        + [pltpu.VMEM(chunks.shape, BF16), pltpu.SemaphoreType.DMA((count + 5 + 3 * count + len(small),))],
        cost_estimate=pl.CostEstimate(
            flops=0, bytes_accessed=6 * both.size + 12 * width * chans, transcendentals=0
        ),
        compiler_params=pltpu.CompilerParams(vmem_limit_bytes=2 * VMEM_LIMIT),
    )(both, in_hbm(chunks))


def mlp_back(normed, w_one, w_two, w_three, cotangent, owners):
    rows, width = normed.shape
    units = w_one.shape[1]
    share = rows // owners
    steps = range(0, width, WIDE)

    def run(normed_ref, one, two, three, cot, parts, out_hbm, grads_hbm, out_parts, grads, sems):
        stores = []

        def store(source, target):
            stores.append(pltpu.make_async_copy(source, target, sems.at[len(stores)]))
            stores[-1].start()

        value, slope = gelu_parts(dot(normed_ref[...], one[...], ((1,), (0,))))
        up = dot(normed_ref[...], two[...], ((1,), (0,)))
        hidden = (value * up).astype(BF16)
        d_hidden = dot(cot[...], three[...], ((1,), (1,)))
        d_gate = (d_hidden * up * slope).astype(BF16)
        d_up = (d_hidden * value).astype(BF16)
        for at in steps:
            cols = slice(at, at + WIDE)
            out = dot(hidden, three[:, cols], ((1,), (0,)))
            out_parts[:, :, cols] = out.astype(BF16).reshape(owners, share, WIDE)
        store(out_parts, out_hbm)
        for at in steps:
            cols = slice(at, at + WIDE)
            grads[cols, :units] = dot(normed_ref[:, cols], d_gate, ((0,), (0,))).astype(BF16)
            grads[cols, units : 2 * units] = dot(normed_ref[:, cols], d_up, ((0,), (0,))).astype(BF16)
            grads[cols, 2 * units :] = dot(cot[:, cols], hidden, ((0,), (0,))).astype(BF16)
            store(grads.at[cols], grads_hbm.at[cols])
        for at in steps:
            cols = slice(at, at + WIDE)
            back = dot(d_gate, one[cols, :], ((1,), (1,))) + dot(d_up, two[cols, :], ((1,), (1,)))
            parts[:, :, cols] = back.astype(BF16).reshape(owners, share, WIDE)
        for copy in stores:
            copy.wait()

    parts = ((owners, share, width), BF16)
    grads = ((width, 3 * units), BF16)
    vmem = pl.BlockSpec(memory_space=pltpu.VMEM)
    anywhere = pl.BlockSpec(memory_space=pl.ANY)
    return pl.pallas_call(
        run,
        name="mlp",
        in_specs=[vmem] * 5,
        out_specs=[vmem, anywhere, anywhere],
        out_shape=[sds(*parts), pltpu.HBM(*parts), pltpu.HBM(*grads)],
        scratch_shapes=[pltpu.VMEM(*parts), pltpu.VMEM(*grads), pltpu.SemaphoreType.DMA((len(steps) + 1,))],
        cost_estimate=pl.CostEstimate(
            flops=18 * rows * width * units, bytes_accessed=14 * width * units, transcendentals=0
        ),
        compiler_params=pltpu.CompilerParams(vmem_limit_bytes=2 * VMEM_LIMIT),
    )(normed, w_one, w_two, w_three, cotangent)


def place_mlp(bundle, units):
    width = bundle.shape[0]

    def run(piece_ref, one_ref, two_ref, three_ref):
        one_ref[...] = piece_ref[:, :units].astype(F32)
        two_ref[...] = piece_ref[:, units : 2 * units].astype(F32)
        three_ref[...] = piece_ref[:, 2 * units :].astype(F32).T

    block = pl.BlockSpec((LANES, units), lambda i: (i, 0))
    return pl.pallas_call(
        run,
        name="place_mlp",
        grid=(width // LANES,),
        in_specs=[pl.BlockSpec((LANES, 3 * units), lambda i: (i, 0))],
        out_specs=[block, block, pl.BlockSpec((units, LANES), lambda i: (0, i))],
        out_shape=[sds((width, units)), sds((width, units)), sds((units, width))],
        cost_estimate=pl.CostEstimate(flops=0, bytes_accessed=18 * width * units, transcendentals=0),
        compiler_params=pltpu.CompilerParams(vmem_limit_bytes=VMEM_LIMIT),
    )(in_hbm(bundle))


def rms(features):
    return lax.rsqrt(jnp.mean(features * features, axis=-1, keepdims=True) + EPS_NORM)


def body(
    tokens,
    cotangent,
    short_lengths,
    long_lengths,
    gain_one,
    gain_two,
    w_y,
    w_x,
    conv_w,
    conv_b,
    gate_a,
    gate_x,
    bias_a,
    bias_x,
    lam,
    w_out,
    w_one,
    w_two,
    w_three,
):
    groups, rows, width = tokens.shape
    chans = w_x.shape[1]
    hidden_units = w_one.shape[1]
    total_rows = groups * rows
    ch_count, ch_index = lax.axis_size("ch"), lax.axis_index("ch")
    seq_count, seq_index = lax.axis_size("seq"), lax.axis_index("seq")
    share_rows = total_rows // ch_count
    share_width = width // ch_count
    start = (seq_index * rows).astype(jnp.int32)[None]
    grouped = lambda a: a.reshape(groups, rows, a.shape[-1])

    tokens = tokens.reshape(total_rows, width)
    cotangent = cotangent.reshape(total_rows, width)
    tokens_f = tokens.astype(F32)
    normed_one, scale_one, conv_input, edge, gate_pre, tokens_share, cotangent_share = front(
        tokens, cotangent, gain_one, w_x.T, w_y.T, groups
    )
    edge = shifted(edge, "seq", 1)

    decay = (-8.0 * jax.nn.softplus(-lam))[None]
    lam_slope = (8.0 * jax.nn.sigmoid(-lam))[None]
    big = sds((groups, rows, chans))
    flops = 2 * total_rows * chans * chans
    keep, decay_run, local_state, carry = run_kernel(
        forward_kernel,
        "conv_gates_scan",
        [big] * 3 + [sds((seq_count, 2, groups, chans))],
        [
            start,
            short_lengths,
            long_lengths,
            conv_input,
            edge,
            conv_w,
            conv_b[None],
            gate_a,
            gate_x,
            bias_a[None],
            bias_x[None],
            decay,
        ],
        [pltpu.VMEM((HALO + rows, chans), F32)],
        flops=2 * flops,
        smem=3,
    )
    state_in = carried_in(carry, False)
    hidden = local_state + decay_run * state_in[:, None]
    mixed_in = (hidden * jax.nn.gelu(gate_pre, approximate=True)).astype(BF16)
    mixed_in = mixed_in.reshape(total_rows, chans)
    share = sds((share_rows, width))
    to_all = sds((ch_count, share_rows, width), BF16)
    resid_share, normed_two = run_kernel(
        mid_kernel,
        "resid_mid_norm",
        [share, to_all],
        [exchange(by_owner(dot(mixed_in, w_out, ((1,), (0,))))), tokens_share, gain_two[None]],
        waits=20,
    )
    normed_two = exchange(normed_two).reshape(total_rows, width)

    two_parts, partial_out, g_mlp = mlp_back(normed_two, w_one, w_two, w_three, cotangent, ch_count)
    d_mid, gain_two_part, d_mix = run_kernel(
        mid_back_kernel,
        "d_mid",
        [share, sds((1, width)), to_all],
        [exchange(two_parts), resid_share, cotangent_share, gain_two[None]],
        after=[g_mlp, partial_out],
        waits=20,
    )
    d_mix = exchange(d_mix).reshape(total_rows, width)
    g_mlp = lax.psum_scatter(g_mlp, "seq", scatter_dimension=0, tiled=True)

    d_mixed = grouped(dot(d_mix, w_out, ((1,), (1,))))
    d_gate_pre, reach, local_adjoint, carry_back = run_kernel(
        adjoint_kernel,
        "adjoint_scan",
        [sds((groups, rows, chans), BF16), big, big, sds((seq_count, 2, groups, chans))],
        [d_mixed, gate_pre, hidden, keep],
        waits=20,
    )
    beyond = carried_in(carry_back, True)
    d_gate_pre = d_gate_pre.reshape(total_rows, chans)
    partial_y = lax.optimization_barrier(dot(d_gate_pre, w_y, ((1,), (1,))))
    d_conv_head, d_input, small, g_mlp = run_kernel(
        gates_back_kernel,
        "gates_back",
        [sds((groups, TAPS - 1, chans)), big, sds((SMALL_ROWS, width))],
        [
            start,
            short_lengths,
            long_lengths,
            local_adjoint,
            reach,
            beyond,
            state_in,
            hidden,
            keep,
            conv_input,
            edge,
            conv_w,
            conv_b[None],
            gate_a,
            gate_x,
            bias_a[None],
            bias_x[None],
            decay,
            lam_slope,
        ],
        [
            pltpu.VMEM((HALO + rows, chans), F32),
            pltpu.VMEM((HALO + rows, chans), F32),
            pltpu.VMEM((rows + HALO, chans), F32),
        ],
        flops=4 * flops,
        smem=3,
        after=[partial_y],
        passed=g_mlp,
        waits=10,
    )
    g_mlp = lax.all_gather(g_mlp, "seq", axis=0, tiled=True)
    lead = shifted(d_conv_head, "seq", -1)
    ahead = start[0] + rows + jnp.arange(TAPS - 1, dtype=jnp.int32)
    lead_masks = []
    for lengths in (short_lengths, long_lengths):
        ends = jnp.cumsum(lengths)
        doc = lambda at: jnp.sum((at[:, None] >= ends[None, :]).astype(jnp.int32), axis=1)
        lead_masks.append(jnp.stack([(doc(ahead) == doc(ahead - k)).astype(F32) for k in range(TAPS)]))
    lead_masks = jnp.stack(lead_masks)
    late = []
    for i in range(TAPS - 1):
        total = jnp.zeros((groups, chans), F32)
        for k in range(TAPS):
            j = i + k - (TAPS - 1)
            if j >= 0:
                total = total + conv_w[k] * lead_masks[:, k, j, None] * lead[:, j]
        late.append(total)
    late = jnp.pad(jnp.stack(late, axis=1), ((0, 0), (rows - TAPS + 1, 0), (0, 0)))
    d_input = (d_input + late).astype(BF16).reshape(total_rows, chans)
    partial_one = dot(d_input, w_x, ((1,), (1,))) + partial_y
    gain_one_part = jnp.sum(partial_one * (tokens_f * scale_one), axis=0, keepdims=True)
    gain_parts = jnp.concatenate([gain_one_part, gain_two_part], axis=0)
    back_pieces = exchange(with_gains([by_owner(partial_one), partial_out], gain_parts))

    padded = lambda a: jnp.pad(a, ((0, 0), (0, -chans % 16)))
    d_gate_wide, mixed_wide = padded(d_gate_pre + 0.0 * d_input), padded(mixed_in + 0.0 * d_input)
    d_input_wide = padded(d_input)

    def terms(other):
        normed_half = half_of(normed_one, 1, other)
        return jnp.concatenate(
            [
                dot(d_gate_wide, normed_half, ((0,), (0,))),
                dot(mixed_wide, half_of(d_mix, 1, other), ((0,), (0,))),
                dot(d_input_wide, normed_half, ((0,), (0,))),
                half_of(small, 1, other),
            ],
            axis=0,
        )

    chunk_parts = reduce_chunk(terms(False), terms(True), 1)

    g_w_one, g_w_two, g_w_three = place_mlp(g_mlp, hidden_units)
    both, chunk = run_kernel(
        tokens_back_kernel,
        "d_tokens",
        [sds((ch_count, 2, share_rows, width), BF16), sds((chunk_parts[0].shape[0] + GAIN_ROWS, LANES), BF16)],
        [back_pieces, Late(tokens_share), Late(resid_share), Late(d_mid), gain_one[None], *chunk_parts],
        after=[g_w_one],
        waits=30,
    )
    (
        d_tokens,
        layer_out,
        g_w_y,
        g_w_out,
        g_w_x,
        g_gate_a,
        g_gate_x,
        g_conv_w,
        g_bias_a,
        g_bias_x,
        g_lam,
        g_conv_b,
        g_gain_one,
        g_gain_two,
    ) = finish(exchange(both), lax.all_gather(chunk, "seq"), chans)
    return (
        layer_out.reshape(groups, rows, width),
        d_tokens.reshape(groups, rows, width),
        g_gain_one[0],
        g_gain_two[0],
        g_w_y.T,
        g_w_x.T,
        g_conv_w,
        g_conv_b[0],
        g_gate_a.transpose(1, 0, 2),
        g_gate_x.transpose(1, 0, 2),
        g_bias_a[0],
        g_bias_x[0],
        g_lam[0],
        g_w_out,
        g_w_one,
        g_w_two,
        g_w_three,
    )


def solution(mesh):
    tokens_spec = P(None, "seq", None)
    column = P(None, "ch")
    block = P("ch", None, None)
    row = P("ch", None)
    vector = P("ch")
    return jax.shard_map(
        body,
        mesh=mesh,
        in_specs=(
            tokens_spec,
            tokens_spec,
            P(),
            P(),
            P(),
            P(),
            column,
            column,
            column,
            vector,
            block,
            block,
            vector,
            vector,
            vector,
            row,
            column,
            column,
            row,
        ),
        out_specs=(
            tokens_spec,
            tokens_spec,
            vector,
            vector,
            column,
            column,
            column,
            vector,
            block,
            block,
            vector,
            vector,
            vector,
            row,
            column,
            column,
            row,
        ),
        check_vma=False,
    )
```

```python
import math

import jax
import jax.numpy as jnp
from jax import lax
from jax.experimental import pallas as pl
from jax.experimental.pallas import tpu as pltpu
from jax.sharding import PartitionSpec as P

EPS_NORM = 1e-06
F32 = jnp.float32
BF16 = jnp.bfloat16
TAPS = 4
VMEM_LIMIT = 16 * 1024 * 1024
LANES = 256
GATE_ROWS = 24
SMALL_ROWS = 64
EARLY = 256
WIDE = 512
GAIN_ROWS = 16
HBM_PER_US = 3_600_000
HALO = 8


def dot(left, right, contract):
    return lax.dot_general(left, right, (contract, ((), ())), preferred_element_type=F32)


def expm1_neg(x):
    series = x * (
        1.0
        + x * (1 / 2)
        * (1.0 + x * (1 / 3) * (1.0 + x * (1 / 4) * (1.0 + x * (1 / 5) * (1.0 + x * (1 / 6) * (1.0 + x * (1 / 7))))))
    )
    return jnp.where(x > -0.35, series, jnp.exp(x) - 1.0)


def doc_masks(ends, count, start, rows):
    positions = start + lax.broadcasted_iota(jnp.int32, (rows, 1), 0)

    def doc(at):
        total = jnp.zeros((rows, 1), jnp.int32)
        for j in range(count):
            total = total + (at >= ends[j]).astype(jnp.int32)
        return total

    here = doc(positions)
    masks = [jnp.ones((rows, 1), F32)]
    for k in range(1, TAPS):
        same = (here == doc(positions - k)) & (positions >= k)
        masks.append(same.astype(F32))
    return masks


def row_ends(length_ref, count):
    ends, total = [], 0
    for j in range(count):
        total = total + length_ref[j]
        ends.append(total)
    return ends


def gates(ext, conv_in, edge, masks, conv_w_ref, conv_b_ref, gate_a_ref, gate_x_ref, bias_a_ref, bias_x_ref):
    rows, chans = conv_in.shape
    ext[HALO - TAPS + 1 : HALO, :] = edge.astype(F32)
    ext[HALO:, :] = conv_in.astype(F32)
    conv_out = jnp.broadcast_to(conv_b_ref[...], (rows, chans))
    for k in range(TAPS):
        conv_out = conv_out + conv_w_ref[k : k + 1, :] * ext[HALO - k : HALO - k + rows, :] * masks[k]
    low = conv_out.astype(BF16)
    rate = jax.nn.sigmoid(dot(low, gate_a_ref[0], ((1,), (0,))) + bias_a_ref[...])
    inlet = jax.nn.sigmoid(dot(low, gate_x_ref[0], ((1,), (0,))) + bias_x_ref[...])
    return conv_out, rate, inlet


def forward_kernel(
    start_ref,
    short_ref,
    long_ref,
    conv_in_ref,
    edge_ref,
    conv_w_ref,
    conv_b_ref,
    gate_a_ref,
    gate_x_ref,
    bias_a_ref,
    bias_x_ref,
    decay_ref,
    keep_ref,
    run_ref,
    state_ref,
    carry_ref,
    ext,
):
    groups, rows, chans = conv_in_ref.shape
    for g in range(groups):
        length_ref = (short_ref, long_ref)[g]
        count = length_ref.shape[0]
        masks = doc_masks(row_ends(length_ref, count), count, start_ref[0], rows)
        conv_out, rate, inlet = gates(
            ext, conv_in_ref[g], edge_ref[g], masks, conv_w_ref, conv_b_ref, gate_a_ref, gate_x_ref, bias_a_ref, bias_x_ref
        )
        log_decay = decay_ref[...] * rate
        keep_ref[g] = jnp.exp(log_decay) * masks[1]
        state_ref[g] = jnp.sqrt(-expm1_neg(2.0 * log_decay)) * inlet * conv_out

    def step(t, carried):
        out = []
        for g in range(groups):
            run, state = carried[g]
            keep = keep_ref[g, pl.ds(t, 1), :]
            run = run * keep
            state = state * keep + state_ref[g, pl.ds(t, 1), :]
            run_ref[g, pl.ds(t, 1), :] = run
            state_ref[g, pl.ds(t, 1), :] = state
            out.append((run, state))
        return tuple(out)

    first = tuple((jnp.ones((1, chans), F32), jnp.zeros((1, chans), F32)) for _ in range(groups))
    last = lax.fori_loop(0, rows, step, first, unroll=8)
    carry = jnp.concatenate([last[g][n] for n in range(2) for g in range(groups)], axis=0)
    for j in range(carry_ref.shape[0]):
        carry_ref[j] = carry


def gelu_parts(x):
    root = 0.7978845608028654
    cubic = 0.044715
    inner = root * (x + cubic * x * x * x)
    th = jnp.tanh(inner)
    half = 0.5 * (1.0 + th)
    slope = half + 0.5 * x * (1.0 - th * th) * root * (1.0 + 3.0 * cubic * x * x)
    return x * half, slope


def adjoint_kernel(
    d_mixed_ref,
    gate_pre_ref,
    hidden_ref,
    keep_ref,
    d_gate_pre_ref,
    reach_ref,
    adj_ref,
    carry_ref,
):
    groups, rows, chans = d_mixed_ref.shape
    for g in range(groups):
        branch, slope = gelu_parts(gate_pre_ref[g])
        d_mixed = d_mixed_ref[g]
        d_gate_pre_ref[g] = (d_mixed * hidden_ref[g] * slope).astype(BF16)
        adj_ref[g] = d_mixed * branch

    def step(i, carried):
        t = rows - 1 - i
        out = []
        for g in range(groups):
            reach, passed = carried[g]
            adj = adj_ref[g, pl.ds(t, 1), :] + passed
            adj_ref[g, pl.ds(t, 1), :] = adj
            reach_ref[g, pl.ds(t, 1), :] = reach
            keep = keep_ref[g, pl.ds(t, 1), :]
            out.append((reach * keep, adj * keep))
        return tuple(out)

    first = tuple((jnp.ones((1, chans), F32), jnp.zeros((1, chans), F32)) for _ in range(groups))
    last = lax.fori_loop(0, rows, step, first, unroll=8)
    carry = jnp.concatenate([last[g][n] for n in range(2) for g in range(groups)], axis=0)
    for j in range(carry_ref.shape[0]):
        carry_ref[j] = carry


def gates_back_kernel(
    midway,
    start_ref,
    short_ref,
    long_ref,
    adj_ref,
    reach_ref,
    beyond_ref,
    state_in_ref,
    hidden_ref,
    keep_ref,
    conv_in_ref,
    edge_ref,
    conv_w_ref,
    conv_b_ref,
    gate_a_ref,
    gate_x_ref,
    bias_a_ref,
    bias_x_ref,
    decay_ref,
    lam_slope_ref,
    d_conv_head_ref,
    d_input_ref,
    small_ref,
    ext,
    prior,
    d_ext,
):
    groups, rows, chans = adj_ref.shape
    sums = [jnp.zeros((1, chans), F32) for _ in range(8)]
    grad_a = grad_x = jnp.zeros((chans, chans), F32)
    for g in range(groups):
        length_ref = (short_ref, long_ref)[g]
        count = length_ref.shape[0]
        ends = row_ends(length_ref, count)
        masks = doc_masks(ends, count, start_ref[0], rows)
        adjoint = adj_ref[g] + reach_ref[g] * beyond_ref[g : g + 1, :]
        prior[HALO - 1 : HALO, :] = state_in_ref[g : g + 1, :]
        prior[HALO:, :] = hidden_ref[g]
        d_keep = adjoint * prior[HALO - 1 : HALO - 1 + rows, :]
        conv_out, rate, inlet = gates(
            ext, conv_in_ref[g], edge_ref[g], masks, conv_w_ref, conv_b_ref, gate_a_ref, gate_x_ref, bias_a_ref, bias_x_ref
        )
        decay = decay_ref[...]
        log_decay = decay * rate
        square = -expm1_neg(2.0 * log_decay)
        root = jnp.sqrt(square)
        driven = adjoint * conv_out
        d_log = d_keep * keep_ref[g] - driven * inlet * (1.0 - square) / root
        d_rate_pre = d_log * decay * rate * (1.0 - rate)
        d_inlet_pre = driven * root * inlet * (1.0 - inlet)
        sums[0] = sums[0] + jnp.sum(d_rate_pre, axis=0, keepdims=True)
        sums[1] = sums[1] + jnp.sum(d_inlet_pre, axis=0, keepdims=True)
        sums[2] = sums[2] + jnp.sum(d_log * rate, axis=0, keepdims=True)
        low = conv_out.astype(BF16)
        low_a = d_rate_pre.astype(BF16)
        low_x = d_inlet_pre.astype(BF16)
        grad_a = grad_a + dot(low, low_a, ((0,), (0,)))
        grad_x = grad_x + dot(low, low_x, ((0,), (0,)))
        d_conv = (
            adjoint * root * inlet
            + dot(low_a, gate_a_ref[0], ((1,), (1,)))
            + dot(low_x, gate_x_ref[0], ((1,), (1,)))
        )
        sums[3] = sums[3] + jnp.sum(d_conv, axis=0, keepdims=True)
        d_input = conv_w_ref[0:1, :] * d_conv
        sums[4] = sums[4] + jnp.sum(d_conv * ext[HALO:, :], axis=0, keepdims=True)
        d_ext[rows:, :] = jnp.zeros((HALO, chans), F32)
        for k in range(1, TAPS):
            masked = d_conv * masks[k]
            sums[4 + k] = sums[4 + k] + jnp.sum(
                masked * ext[HALO - k : HALO - k + rows, :], axis=0, keepdims=True
            )
            d_ext[:rows, :] = masked
            d_input = d_input + conv_w_ref[k : k + 1, :] * d_ext[k : k + rows, :]
        d_input_ref[g] = d_input
        d_conv_head_ref[g] = d_conv[: TAPS - 1, :]
        if g == 0:
            midway()
    sums[2] = sums[2] * lam_slope_ref[...]
    small_ref[...] = jnp.zeros(small_ref.shape, F32)
    for i, total in enumerate(sums):
        lanes = slice(LANES * i, LANES * i + chans)
        first, last = GATE_ROWS * i, min(GATE_ROWS * (i + 1), chans)
        small_ref[: last - first, lanes] = grad_a[first:last]
        small_ref[GATE_ROWS : GATE_ROWS + last - first, lanes] = grad_x[first:last]
        small_ref[2 * GATE_ROWS : 2 * GATE_ROWS + 1, lanes] = total


def sds(shape, dtype=F32):
    return jax.ShapeDtypeStruct(shape, dtype)


def in_hbm(array):
    return pltpu.with_memory_space_constraint(array, pltpu.HBM)


class Late:
    def __init__(self, array, share=0):
        self.array, self.share = in_hbm(array), share
        self.held = pltpu.VMEM((share or array.shape[0],) + array.shape[1:], array.dtype)

    def source(self, ref):
        if not self.share:
            return ref
        at = pl.multiple_of(lax.axis_index("ch") * self.share, self.share)
        return ref.at[pl.ds(at, self.share)]


class Arriving:
    def __init__(self, copy, ref):
        self.copy, self.ref, self.shape = copy, ref, ref.shape
        copy.start()

    def wait(self):
        if self.copy is not None:
            self.copy.wait()
            self.copy = None

    def __getitem__(self, index):
        self.wait()
        return self.ref[index]


def run_kernel(kernel, name, outs, ins, scratch=(), flops=0, smem=0, after=(), passed=None, waits=0):
    vmem = pl.BlockSpec(memory_space=pltpu.VMEM)
    scalar = pl.BlockSpec(memory_space=pltpu.SMEM)
    anywhere = pl.BlockSpec(memory_space=pl.ANY)
    late = [a if isinstance(a, Late) else None for a in ins]
    ins = [a.array if isinstance(a, Late) else a for a in ins]
    moved = sum(a.size * a.dtype.itemsize for a in list(ins) + list(outs))
    count, skip = len(ins), len(after)
    in_specs = [scalar] * smem + [anywhere if l else vmem for l in late[smem:]] + [anywhere] * skip
    held = [l.held for l in late if l]
    ins = [*ins, *[in_hbm(a) for a in after]]
    out_specs = [vmem] * len(outs)
    outs, scratch = list(outs), list(scratch)
    if passed is not None:
        ins.append(in_hbm(passed))
        in_specs.append(anywhere)
        outs.append(pltpu.HBM(passed.shape, passed.dtype))
        out_specs.append(anywhere)
        scratch += [pltpu.VMEM(passed.shape, passed.dtype), pltpu.SemaphoreType.DMA((2,))]

    def run(*refs):
        if held:
            refs, arrived, sems = list(refs[: -len(held) - 1]), refs[-len(held) - 1 : -1], refs[-1]
            for n, i in enumerate([i for i in range(count) if late[i]]):
                source = late[i].source(refs[i])
                refs[i] = Arriving(pltpu.make_async_copy(source, arrived[n], sems.at[n]), arrived[n])
        if passed is None:
            kernel(*refs[:count], *refs[count + skip :])
            for ref in refs[:count]:
                if isinstance(ref, Arriving):
                    ref.wait()
            return
        in_ref, out_ref = refs[count + skip], refs[count + skip + len(outs)]
        buffer, both_sems = refs[-2:]
        fetch = pltpu.make_async_copy(in_ref, buffer, both_sems.at[0])
        store = pltpu.make_async_copy(buffer, out_ref, both_sems.at[1])
        fetch.start()

        def midway():
            fetch.wait()
            store.start()

        kept = refs[count + skip + 1 : count + skip + len(outs)]
        kernel(midway, *refs[:count], *kept, *refs[count + skip + len(outs) + 1 : -2])
        store.wait()

    return pl.pallas_call(
        run,
        name=name,
        out_shape=outs,
        in_specs=in_specs,
        out_specs=out_specs,
        scratch_shapes=scratch + ([*held, pltpu.SemaphoreType.DMA((len(held),))] if held else []),
        cost_estimate=pl.CostEstimate(flops=flops, bytes_accessed=moved + waits * HBM_PER_US, transcendentals=0),
        compiler_params=pltpu.CompilerParams(vmem_limit_bytes=VMEM_LIMIT),
    )(*ins)


def front(tokens, cotangent, gain, w_x, w_y, groups):
    total, width = tokens.shape
    share = total // lax.axis_size("ch")
    chans = w_x.shape[0]
    rows = total // groups
    step = total // 4

    def run(*refs):
        gain_hbm, sources, outs, held, kept, sems = refs[0], refs[1:5], refs[5:12], refs[12:14], refs[14:18], refs[18]
        normed_out, scale_ref, conv_in_ref, edge_ref, gate_out, tokens_share_ref, cot_share_ref = outs
        gain_ref = Arriving(pltpu.make_async_copy(gain_hbm, kept[3], sems.at[12]), kept[3])
        tokens_ref, normed_ref, gate_ref, _ = kept
        reads = []
        for n in range(4):
            part = pl.ds(n * step, step)
            reads.append(pltpu.make_async_copy(sources[0].at[part], tokens_ref.at[part], sems.at[n]))
            reads[-1].start()
        w_x_ref, w_y_ref = [
            Arriving(pltpu.make_async_copy(source, ref, sems.at[4 + n]), ref)
            for n, (source, ref) in enumerate(zip(sources[1:3], held))
        ]
        mine = pl.ds(pl.multiple_of(lax.axis_index("ch") * share, share), share)
        cot_share = pltpu.make_async_copy(sources[3].at[mine], cot_share_ref, sems.at[11])
        cot_share.start()
        stores = [cot_share]
        for n in range(4):
            reads[n].wait()
            for at in range(n * step, (n + 1) * step, 32):
                part = slice(at, at + 32)
                features = tokens_ref[part, :].astype(F32)
                scale = rms(features)
                scale_ref[part, :] = scale
                normed_ref[part, :] = (features * scale * gain_ref[...]).astype(BF16)
            part = pl.ds(n * step, step)
            stores.append(pltpu.make_async_copy(normed_ref.at[part], normed_out.at[part], sems.at[6 + n]))
            stores[-1].start()
        tokens_share_ref[...] = tokens_ref[mine, :]
        for g in range(groups):
            part = normed_ref[g * rows : (g + 1) * rows, :]
            gate_ref[g] = dot(part, w_y_ref[...], ((1,), (1,)))
        stores.append(pltpu.make_async_copy(gate_ref, gate_out, sems.at[10]))
        stores[-1].start()
        for g in range(groups):
            part = normed_ref[g * rows : (g + 1) * rows, :]
            conv_in = dot(part, w_x_ref[...], ((1,), (1,))).astype(BF16)
            conv_in_ref[g] = conv_in
            edge_ref[g] = conv_in[rows - TAPS + 1 :, :]
        for store in stores:
            store.wait()

    vmem = pl.BlockSpec(memory_space=pltpu.VMEM)
    anywhere = pl.BlockSpec(memory_space=pl.ANY)
    return pl.pallas_call(
        run,
        name="front",
        in_specs=[anywhere] * 5,
        out_specs=[anywhere, vmem, vmem, vmem, anywhere, vmem, vmem],
        out_shape=[
            pltpu.HBM((total, width), BF16),
            sds((total, 1)),
            sds((groups, rows, chans), BF16),
            sds((groups, TAPS - 1, chans), BF16),
            pltpu.HBM((groups, rows, chans), F32),
            sds((share, width), BF16),
            sds((share, width), BF16),
        ],
        scratch_shapes=[
            pltpu.VMEM(w_x.shape, BF16),
            pltpu.VMEM(w_y.shape, BF16),
            pltpu.VMEM((total, width), BF16),
            pltpu.VMEM((total, width), BF16),
            pltpu.VMEM((groups, rows, chans), F32),
            pltpu.VMEM((1, width), F32),
            pltpu.SemaphoreType.DMA((13,)),
        ],
        cost_estimate=pl.CostEstimate(
            flops=4 * total * chans * width, bytes_accessed=4 * total * width, transcendentals=0
        ),
        compiler_params=pltpu.CompilerParams(vmem_limit_bytes=VMEM_LIMIT),
    )(in_hbm(gain[None]), in_hbm(tokens), in_hbm(w_x), in_hbm(w_y), in_hbm(cotangent))


def shifted(block, axis, distance):
    count = lax.axis_size(axis)
    route = [(i - distance, i) for i in range(count) if 0 <= i - distance < count]
    return lax.ppermute(block, axis, route)


def carried_in(value, backward):
    count, mine = lax.axis_size("seq"), lax.axis_index("seq")
    pieces = lax.all_to_all(value, "seq", 0, 0)
    groups = value.shape[1] // 2
    total = jnp.zeros((groups, value.shape[2]), F32)
    for j in range(count - 1, 0, -1) if backward else range(count - 1):
        longer = pieces[j, groups:] + pieces[j, :groups] * total
        total = jnp.where((j > mine) if backward else (j < mine), longer, total)
    return total


def sum_parts(got_ref):
    total = got_ref[0].astype(F32)
    for j in range(1, got_ref.shape[0]):
        total = total + got_ref[j].astype(F32)
    return total


def send_to_all(out_ref, share):
    share = share.astype(BF16)
    for j in range(out_ref.shape[0]):
        out_ref[j] = share


def norm_back(features, gain, grad):
    scale = rms(features)
    gained = gain * grad
    mean = jnp.mean(gained * features, axis=-1, keepdims=True)
    back = scale * gained - features * (scale * scale * scale) * mean
    return back, jnp.sum(grad * (features * scale), axis=0, keepdims=True)


def mid_kernel(got_ref, tokens_ref, gain_ref, resid_ref, normed_ref):
    resid = tokens_ref[...].astype(F32) + sum_parts(got_ref)
    resid_ref[...] = resid
    send_to_all(normed_ref, resid * rms(resid) * gain_ref[...])


def mid_back_kernel(got_ref, resid_ref, cotangent_ref, gain_ref, d_mid_ref, g_gain_ref, early_ref, d_mix_ref):
    width = resid_ref.shape[1]
    total = sum_parts(got_ref)
    resid = resid_ref[...]
    early_ref[...] = (resid[:, :EARLY] + total[:, width:]).astype(BF16)
    back, g_gain = norm_back(resid, gain_ref[...], total[:, :width])
    d_mid = cotangent_ref[...].astype(F32) + back
    d_mid_ref[...] = d_mid
    g_gain_ref[...] = g_gain
    send_to_all(d_mix_ref, d_mid)


def exchange(pieces):
    return lax.all_to_all(pieces, "ch", 0, 0)


def by_owner(partial_sum):
    count = lax.axis_size("ch")
    rows, width = partial_sum.shape
    return partial_sum.astype(BF16).reshape(count, rows // count, width)


def with_gains(pieces, gains):
    count, share, width = pieces[0].shape
    more = gains.astype(BF16).reshape(-1, count, width // count).swapaxes(0, 1)
    more = jnp.pad(more, ((0, 0), (0, share - gains.shape[0]), (0, 0)))
    return jnp.concatenate([*pieces, more], axis=-1)


def seq_route(fn):
    count = lax.axis_size("seq")
    return [(i, fn(i) % count) for i in range(count)]


def swap_core(value):
    return lax.ppermute(value, "seq", seq_route(lambda i: i ^ 1))


def shift_z(value, hops):
    return lax.ppermute(value, "seq", seq_route(lambda i: i + 2 * hops))


def half_of(array, axis, other):
    core = lax.axis_index("seq") % 2
    size = array.shape[axis] // 2
    return lax.dynamic_slice_in_dim(array, ((1 - core) if other else core) * size, size, axis)


def reduce_chunk(kept, sent, axis):
    z = lax.axis_index("seq") // 2
    got = swap_core(sent.astype(BF16))
    size = kept.shape[axis] // 4

    def piece(hops):
        at = ((z + hops) % 4) * size
        cut = lambda a: lax.dynamic_slice_in_dim(a, at, size, axis).astype(F32)
        return (cut(kept) + cut(got)).astype(BF16)

    return [piece(0)] + [shift_z(piece(hops), hops) for hops in (1, 3, 2)]


def tokens_back(got, tokens, resid, early, d_mid, gain, chunk_parts, after):
    owners, share, _ = got.shape
    width = tokens.shape[1]
    rows, lanes = chunk_parts[0].shape
    late = [in_hbm(a) for a in (tokens, resid, early, d_mid, *chunk_parts)]
    count = len(late)

    def run(got_ref, gain_ref, *refs):
        sources, (both_hbm, sent_ref) = refs[:count], refs[count + 1 : count + 3]
        held, block, sems = refs[count + 3 : 2 * count + 3], refs[-2], refs[-1]
        tokens_ref, resid_ref, early_ref, d_mid_ref, *part_refs = [
            Arriving(pltpu.make_async_copy(source, ref, sems.at[n]), ref)
            for n, (source, ref) in enumerate(zip(sources, held))
        ]
        stores = []

        def send(which):
            for j in range(owners):
                stores.append(
                    pltpu.make_async_copy(block.at[which], both_hbm.at[j, which], sems.at[count + len(stores)])
                )
                stores[-1].start()

        def total(at, size):
            cols = slice(at, at + size)
            result = got_ref[0, :, cols].astype(F32)
            for j in range(1, owners):
                result = result + got_ref[j, :, cols].astype(F32)
            return result

        grad = total(0, width)
        back, _ = norm_back(tokens_ref[...].astype(F32), gain_ref[...], grad)
        block[0] = (d_mid_ref[...] + back).astype(BF16)
        send(0)
        block[1, :, :EARLY] = early_ref[...]
        block[1, :, EARLY:] = (resid_ref[:, EARLY:] + total(width, width - EARLY)).astype(BF16)
        send(1)
        gains = total(2 * width - EARLY, width // owners)[:GAIN_ROWS]
        chunk = part_refs[0][...].astype(F32)
        for part_ref in part_refs[1:]:
            chunk = chunk + part_ref[...].astype(F32)
        sent_ref[:rows, :] = chunk.astype(BF16)
        sent_ref[rows:, : width // owners] = gains.astype(BF16)
        sent_ref[rows:, width // owners :] = jnp.zeros((GAIN_ROWS, lanes - width // owners), BF16)
        for store in stores:
            store.wait()

    vmem = pl.BlockSpec(memory_space=pltpu.VMEM)
    anywhere = pl.BlockSpec(memory_space=pl.ANY)
    return pl.pallas_call(
        run,
        name="d_tokens",
        in_specs=[vmem] * 2 + [anywhere] * (count + 1),
        out_specs=[anywhere, vmem],
        out_shape=[pltpu.HBM((owners, 2, share, width), BF16), sds((rows + GAIN_ROWS, lanes), BF16)],
        scratch_shapes=[pltpu.VMEM(a.shape, a.dtype) for a in late]
        + [pltpu.VMEM((2, share, width), BF16), pltpu.SemaphoreType.DMA((count + 2 * owners,))],
        cost_estimate=pl.CostEstimate(flops=0, bytes_accessed=2 * got.size, transcendentals=0),
        compiler_params=pltpu.CompilerParams(vmem_limit_bytes=VMEM_LIMIT),
    )(got, gain, *late, in_hbm(after))


def finish(both, chunks, chans):
    owners, _, share, width = both.shape
    count = chunks.shape[0]
    wide = (chunks.shape[1] - SMALL_ROWS - GAIN_ROWS) // 3
    step = owners // 4
    gain_width = width // owners

    def run(both_ref, chunks_hbm, *refs):
        outs, kept, chunk_ref, sems = refs[:14], refs[14:27], refs[27], refs[28]
        d_tokens_hbm, layer_hbm = outs[:2]
        d_tokens_ref, y_ref, out_ref, x_ref, gate_a_ref, gate_x_ref, conv_w_ref, *rows_refs = kept
        *rows_refs, gain_one_ref, gain_two_ref = rows_refs
        reads, stores = [], []

        def store(source, target):
            stores.append(pltpu.make_async_copy(source, target, sems.at[count + len(stores)]))
            stores[-1].start()

        for i in range(count):
            reads.append(pltpu.make_async_copy(chunks_hbm.at[i], chunk_ref.at[i], sems.at[i]))
            reads[-1].start()
        store(both_ref.at[:, 1], layer_hbm)
        for n in range(4):
            part = slice(n * step, (n + 1) * step)
            d_tokens_ref[part] = both_ref[part, 0].astype(F32)
            store(d_tokens_ref.at[pl.ds(n * step, step)], d_tokens_hbm.at[pl.ds(n * step, step)])
        gains = jnp.zeros((8, LANES), F32)
        for i in range(count):
            chunk = i % 2 * 4 + i // 2
            lanes = pl.ds(chunk * LANES, LANES)
            reads[i].wait()
            for n, (ref, hbm) in enumerate(zip((y_ref, out_ref, x_ref), outs[2:5])):
                ref[:, chunk * LANES : (chunk + 1) * LANES] = chunk_ref[i, n * wide : n * wide + chans, :].astype(F32)
                store(ref.at[:, lanes], hbm.at[:, lanes])
            small = chunk_ref[i, 3 * wide :, :].astype(F32)
            for n, ref in enumerate((gate_a_ref, gate_x_ref)):
                for r in range(min(GATE_ROWS, chans - chunk * GATE_ROWS)):
                    ref[chunk * GATE_ROWS + r] = small[n * GATE_ROWS + r : n * GATE_ROWS + r + 1, :chans]
            total = small[2 * GATE_ROWS : 2 * GATE_ROWS + 1, :chans]
            if chunk < 4:
                rows_refs[chunk][...] = total
            else:
                conv_w_ref[chunk - 4 : chunk - 3, :] = total
            gains = gains + small[SMALL_ROWS : SMALL_ROWS + 8]
        gain_one_ref[...] = gains[0:1, :gain_width]
        gain_two_ref[...] = gains[1:2, :gain_width]
        for source, target in zip(kept[4:], outs[5:]):
            store(source, target)
        for copy in stores:
            copy.wait()

    weight = ((chans, width), F32)
    gate = ((chans, 1, chans), F32)
    row = ((1, chans), F32)
    gain = ((1, gain_width), F32)
    blocks = ((owners, share, width), F32)
    small = [gate, gate, ((TAPS, chans), F32), row, row, row, row, gain, gain]
    anywhere = pl.BlockSpec(memory_space=pl.ANY)
    return pl.pallas_call(
        run,
        name="finish",
        in_specs=[pl.BlockSpec(memory_space=pltpu.VMEM), anywhere],
        out_specs=[anywhere] * 14,
        out_shape=[pltpu.HBM(*out) for out in (blocks, (blocks[0], BF16), weight, weight, weight, *small)],
        scratch_shapes=[pltpu.VMEM(*out) for out in (blocks, weight, weight, weight, *small)]
        + [pltpu.VMEM(chunks.shape, BF16), pltpu.SemaphoreType.DMA((count + 5 + 3 * count + len(small),))],
        cost_estimate=pl.CostEstimate(
            flops=0, bytes_accessed=6 * both.size + 12 * width * chans, transcendentals=0
        ),
        compiler_params=pltpu.CompilerParams(vmem_limit_bytes=2 * VMEM_LIMIT),
    )(both, in_hbm(chunks))


def mlp_back(normed, w_one, w_two, w_three, cotangent, owners):
    rows, width = normed.shape
    units = w_one.shape[1]
    share = rows // owners
    steps = range(0, width, WIDE)

    def run(normed_ref, one, two, three, cot, parts, out_hbm, grads_hbm, out_parts, grads, sems):
        stores = []

        def store(source, target):
            stores.append(pltpu.make_async_copy(source, target, sems.at[len(stores)]))
            stores[-1].start()

        value, slope = gelu_parts(dot(normed_ref[...], one[...], ((1,), (0,))))
        up = dot(normed_ref[...], two[...], ((1,), (0,)))
        hidden = (value * up).astype(BF16)
        d_hidden = dot(cot[...], three[...], ((1,), (1,)))
        d_gate = (d_hidden * up * slope).astype(BF16)
        d_up = (d_hidden * value).astype(BF16)
        for at in steps:
            cols = slice(at, at + WIDE)
            out = dot(hidden, three[:, cols], ((1,), (0,))).astype(BF16).reshape(owners, share, WIDE)
            early = max(EARLY - at, 0)
            if early:
                parts[:, :, width + at : width + EARLY] = out[:, :, :early]
            out_parts[:, :, max(at - EARLY, 0) : at - EARLY + WIDE] = out[:, :, early:]
        store(out_parts, out_hbm)
        for at in steps:
            cols = slice(at, at + WIDE)
            grads[cols, :units] = dot(normed_ref[:, cols], d_gate, ((0,), (0,))).astype(BF16)
            grads[cols, units : 2 * units] = dot(normed_ref[:, cols], d_up, ((0,), (0,))).astype(BF16)
            grads[cols, 2 * units :] = dot(cot[:, cols], hidden, ((0,), (0,))).astype(BF16)
            store(grads.at[cols], grads_hbm.at[cols])
        for at in steps:
            cols = slice(at, at + WIDE)
            back = dot(d_gate, one[cols, :], ((1,), (1,))) + dot(d_up, two[cols, :], ((1,), (1,)))
            parts[:, :, cols] = back.astype(BF16).reshape(owners, share, WIDE)
        for copy in stores:
            copy.wait()

    parts = ((owners, share, width + EARLY), BF16)
    later = ((owners, share, width - EARLY), BF16)
    grads = ((width, 3 * units), BF16)
    vmem = pl.BlockSpec(memory_space=pltpu.VMEM)
    anywhere = pl.BlockSpec(memory_space=pl.ANY)
    return pl.pallas_call(
        run,
        name="mlp",
        in_specs=[vmem] * 5,
        out_specs=[vmem, anywhere, anywhere],
        out_shape=[sds(*parts), pltpu.HBM(*later), pltpu.HBM(*grads)],
        scratch_shapes=[pltpu.VMEM(*later), pltpu.VMEM(*grads), pltpu.SemaphoreType.DMA((len(steps) + 1,))],
        cost_estimate=pl.CostEstimate(
            flops=18 * rows * width * units, bytes_accessed=14 * width * units, transcendentals=0
        ),
        compiler_params=pltpu.CompilerParams(vmem_limit_bytes=2 * VMEM_LIMIT),
    )(normed, w_one, w_two, w_three, cotangent)


def place_mlp(bundle, units):
    width = bundle.shape[0]

    def run(piece_ref, one_ref, two_ref, three_ref):
        one_ref[...] = piece_ref[:, :units].astype(F32)
        two_ref[...] = piece_ref[:, units : 2 * units].astype(F32)
        three_ref[...] = piece_ref[:, 2 * units :].astype(F32).T

    block = pl.BlockSpec((LANES, units), lambda i: (i, 0))
    return pl.pallas_call(
        run,
        name="place_mlp",
        grid=(width // LANES,),
        in_specs=[pl.BlockSpec((LANES, 3 * units), lambda i: (i, 0))],
        out_specs=[block, block, pl.BlockSpec((units, LANES), lambda i: (0, i))],
        out_shape=[sds((width, units)), sds((width, units)), sds((units, width))],
        cost_estimate=pl.CostEstimate(flops=0, bytes_accessed=18 * width * units, transcendentals=0),
        compiler_params=pltpu.CompilerParams(vmem_limit_bytes=VMEM_LIMIT),
    )(in_hbm(bundle))


def rms(features):
    return lax.rsqrt(jnp.mean(features * features, axis=-1, keepdims=True) + EPS_NORM)


def body(
    tokens,
    cotangent,
    short_lengths,
    long_lengths,
    gain_one,
    gain_two,
    w_y,
    w_x,
    conv_w,
    conv_b,
    gate_a,
    gate_x,
    bias_a,
    bias_x,
    lam,
    w_out,
    w_one,
    w_two,
    w_three,
):
    groups, rows, width = tokens.shape
    chans = w_x.shape[1]
    hidden_units = w_one.shape[1]
    total_rows = groups * rows
    ch_count, ch_index = lax.axis_size("ch"), lax.axis_index("ch")
    seq_count, seq_index = lax.axis_size("seq"), lax.axis_index("seq")
    share_rows = total_rows // ch_count
    share_width = width // ch_count
    start = (seq_index * rows).astype(jnp.int32)[None]
    grouped = lambda a: a.reshape(groups, rows, a.shape[-1])

    tokens = tokens.reshape(total_rows, width)
    cotangent = cotangent.reshape(total_rows, width)
    tokens_f = tokens.astype(F32)
    normed_one, scale_one, conv_input, edge, gate_pre, tokens_share, cotangent_share = front(
        tokens, cotangent, gain_one, w_x.T, w_y.T, groups
    )
    edge = shifted(edge, "seq", 1)

    decay = (-8.0 * jax.nn.softplus(-lam))[None]
    lam_slope = (8.0 * jax.nn.sigmoid(-lam))[None]
    big = sds((groups, rows, chans))
    flops = 2 * total_rows * chans * chans
    keep, decay_run, local_state, carry = run_kernel(
        forward_kernel,
        "conv_gates_scan",
        [big] * 3 + [sds((seq_count, 2 * groups, chans))],
        [
            start,
            short_lengths,
            long_lengths,
            conv_input,
            edge,
            conv_w,
            conv_b[None],
            gate_a,
            gate_x,
            bias_a[None],
            bias_x[None],
            decay,
        ],
        [pltpu.VMEM((HALO + rows, chans), F32)],
        flops=2 * flops,
        smem=3,
    )
    state_in = carried_in(carry, False)
    hidden = local_state + decay_run * state_in[:, None]
    mixed_in = (hidden * jax.nn.gelu(gate_pre, approximate=True)).astype(BF16)
    mixed_in = mixed_in.reshape(total_rows, chans)
    share = sds((share_rows, width))
    to_all = sds((ch_count, share_rows, width), BF16)
    resid_share, normed_two = run_kernel(
        mid_kernel,
        "resid_mid_norm",
        [share, to_all],
        [exchange(by_owner(dot(mixed_in, w_out, ((1,), (0,))))), tokens_share, gain_two[None]],
        waits=20,
    )
    normed_two = exchange(normed_two).reshape(total_rows, width)

    two_parts, partial_out, g_mlp = mlp_back(normed_two, w_one, w_two, w_three, cotangent, ch_count)
    d_mid, gain_two_part, early, d_mix = run_kernel(
        mid_back_kernel,
        "d_mid",
        [share, sds((1, width)), sds((share_rows, EARLY), BF16), to_all],
        [exchange(two_parts), resid_share, cotangent_share, gain_two[None]],
        after=[g_mlp, partial_out],
        waits=20,
    )
    d_mix = exchange(d_mix).reshape(total_rows, width)
    g_mlp = lax.psum_scatter(g_mlp, "seq", scatter_dimension=0, tiled=True)

    d_mixed = grouped(dot(d_mix, w_out, ((1,), (1,))))
    d_gate_pre, reach, local_adjoint, carry_back = run_kernel(
        adjoint_kernel,
        "adjoint_scan",
        [sds((groups, rows, chans), BF16), big, big, sds((seq_count, 2 * groups, chans))],
        [d_mixed, gate_pre, hidden, keep],
        waits=20,
    )
    beyond = carried_in(carry_back, True)
    d_conv_head, d_input, small, g_mlp = run_kernel(
        gates_back_kernel,
        "gates_back",
        [sds((groups, TAPS - 1, chans)), big, sds((SMALL_ROWS, width))],
        [
            start,
            short_lengths,
            long_lengths,
            local_adjoint,
            reach,
            beyond,
            state_in,
            hidden,
            keep,
            conv_input,
            edge,
            conv_w,
            conv_b[None],
            gate_a,
            gate_x,
            bias_a[None],
            bias_x[None],
            decay,
            lam_slope,
        ],
        [
            pltpu.VMEM((HALO + rows, chans), F32),
            pltpu.VMEM((HALO + rows, chans), F32),
            pltpu.VMEM((rows + HALO, chans), F32),
        ],
        flops=4 * flops,
        smem=3,
        passed=g_mlp,
        waits=10,
    )
    g_mlp = lax.all_gather(g_mlp, "seq", axis=0, tiled=True)
    lead = shifted(d_conv_head, "seq", -1)
    ahead = start[0] + rows + jnp.arange(TAPS - 1, dtype=jnp.int32)
    lead_masks = []
    for lengths in (short_lengths, long_lengths):
        ends = jnp.cumsum(lengths)
        doc = lambda at: jnp.sum((at[:, None] >= ends[None, :]).astype(jnp.int32), axis=1)
        lead_masks.append(jnp.stack([(doc(ahead) == doc(ahead - k)).astype(F32) for k in range(TAPS)]))
    lead_masks = jnp.stack(lead_masks)
    late = []
    for i in range(TAPS - 1):
        total = jnp.zeros((groups, chans), F32)
        for k in range(TAPS):
            j = i + k - (TAPS - 1)
            if j >= 0:
                total = total + conv_w[k] * lead_masks[:, k, j, None] * lead[:, j]
        late.append(total)
    late = jnp.pad(jnp.stack(late, axis=1), ((0, 0), (rows - TAPS + 1, 0), (0, 0)))
    d_input = (d_input + late).astype(BF16).reshape(total_rows, chans)
    d_gate_pre = d_gate_pre.reshape(total_rows, chans)

    partial_one = dot(d_input, w_x, ((1,), (1,))) + dot(d_gate_pre, w_y, ((1,), (1,)))
    gain_one_part = jnp.sum(partial_one * (tokens_f * scale_one), axis=0, keepdims=True)
    gain_parts = jnp.concatenate([gain_one_part, gain_two_part], axis=0)
    back_pieces = exchange(with_gains([by_owner(partial_one), partial_out], gain_parts))

    padded = lambda a: jnp.pad(a, ((0, 0), (0, -chans % 16)))
    d_gate_wide, mixed_wide = padded(d_gate_pre + 0.0 * d_input), padded(mixed_in + 0.0 * d_input)
    d_input_wide = padded(d_input)

    def terms(other):
        normed_half = half_of(normed_one, 1, other)
        return jnp.concatenate(
            [
                dot(d_gate_wide, normed_half, ((0,), (0,))),
                dot(mixed_wide, half_of(d_mix, 1, other), ((0,), (0,))),
                dot(d_input_wide, normed_half, ((0,), (0,))),
                half_of(small, 1, other),
            ],
            axis=0,
        )

    chunk_parts = reduce_chunk(terms(False), terms(True), 1)

    g_w_one, g_w_two, g_w_three = place_mlp(g_mlp, hidden_units)
    both, chunk = tokens_back(
        back_pieces, tokens_share, resid_share, early, d_mid, gain_one[None], chunk_parts, g_w_one
    )
    (
        d_tokens,
        layer_out,
        g_w_y,
        g_w_out,
        g_w_x,
        g_gate_a,
        g_gate_x,
        g_conv_w,
        g_bias_a,
        g_bias_x,
        g_lam,
        g_conv_b,
        g_gain_one,
        g_gain_two,
    ) = finish(exchange(both), lax.all_gather(chunk, "seq"), chans)
    return (
        layer_out.reshape(groups, rows, width),
        d_tokens.reshape(groups, rows, width),
        g_gain_one[0],
        g_gain_two[0],
        g_w_y.T,
        g_w_x.T,
        g_conv_w,
        g_conv_b[0],
        g_gate_a.transpose(1, 0, 2),
        g_gate_x.transpose(1, 0, 2),
        g_bias_a[0],
        g_bias_x[0],
        g_lam[0],
        g_w_out,
        g_w_one,
        g_w_two,
        g_w_three,
    )


def solution(mesh):
    tokens_spec = P(None, "seq", None)
    column = P(None, "ch")
    block = P("ch", None, None)
    row = P("ch", None)
    vector = P("ch")
    return jax.shard_map(
        body,
        mesh=mesh,
        in_specs=(
            tokens_spec,
            tokens_spec,
            P(),
            P(),
            P(),
            P(),
            column,
            column,
            column,
            vector,
            block,
            block,
            vector,
            vector,
            vector,
            row,
            column,
            column,
            row,
        ),
        out_specs=(
            tokens_spec,
            tokens_spec,
            vector,
            vector,
            column,
            column,
            column,
            vector,
            block,
            block,
            vector,
            vector,
            vector,
            row,
            column,
            column,
            row,
        ),
        check_vma=False,
    )
```
